32 devices in a mesh: groups: 2 (over x), row: 16 (over z, y, core).
Axes of the slice: x: 2, y: 2, z: 4, core: 2. Of those that a mesh axis runs over, the one named last changes fastest.
Arguments:
- pair: bfloat16 [320, 160, 128], P(('groups', 'row')), parts along dimension 0, may hold values from -6 to 6
- mask: int32 [320], P('groups'), parts along dimension 0, may hold values 0 or 1
- chain: int32 [320], P('groups'), parts along dimension 0, may hold values from 0 to 5, never falling along the last dimension, each value on 1 to 53 neighbouring positions
- tri_proj: bfloat16 [128, 512], replicated, may hold values from -0.5 to 0.5
- tri_gate: bfloat16 [128, 128], replicated, may hold values from -0.5 to 0.5
- tri_out: bfloat16 [128, 128], replicated, may hold values from -0.5 to 0.5
- att_proj: bfloat16 [128, 512], replicated, may hold values from -0.5 to 0.5
- att_bias: float32 [128, 4], replicated, may hold values from -23.864854 to 23.864854
- same_chain: float32 [4], replicated, may hold values from -2 to 2
- att_out: bfloat16 [128, 128], replicated, may hold values from -0.26367188 to 0.26367188
Outputs:
- updated: bfloat16 [320, 160, 128], P(('groups', 'row')), parts along dimension 0
The draws below stay inside these ranges and needn't reach their ends.
There are 2 independent parts, one for each index of `groups`. The reference program is written for one: setup_inputs(seed, part) draws one part's arguments, and reference() takes and returns one part's arrays. A program takes and returns all parts, laid end to end along the dimension named above; an argument that names none is the same for every part. Nothing has to cross between parts.
Inputs may be any that keep to these rules, and one draw needn't show every extreme that they name: `mask`: 1 marks a resolved token, 0 a missing one. chain number of each token; each chain is one contiguous run of at most 53 tokens, numbers never falling along the tokens.
All inputs are finite; a program needn't handle non-finite values.
Results may differ from the reference program's by a relative error of at most 0.013.
Values may be sent and summed in bfloat16 or wider, within the bound.
A program may use at most 128 MiB of HBM per device.

```python
import math
import jax
import jax.numpy as jnp
import numpy as np
from jax import lax

C = 128
H = 4
N = 160


def draw_att_bias(key, part):
    base = jnp.clip(jax.random.normal(jax.random.fold_in(key, 11), (C, H), jnp.float32), -6.0, 6.0)
    base = base * (1.5 / math.sqrt(C))
    return base


def plant(values, stream_key, smallest, high):
    longest = values.shape.index(max(values.shape))
    spots = []
    for shift in (0, 1):
        where = [jax.random.randint(jax.random.fold_in(stream_key, axis), (), 0, length) for axis, length in enumerate(values.shape)]
        where[longest] = (where[longest] + shift) % values.shape[longest]
        spots.append(tuple(where))
    return values.at[spots[0]].set(smallest).at[spots[1]].set(high)


def levels(own_key, shape, split, smallest, high):
    loudness, own = 1.0, jax.random.fold_in(own_key, 6)
    for axis_at, shards_of in split:
        draws = jnp.exp(jax.random.uniform(jax.random.fold_in(own, axis_at), (shards_of,), jnp.float32, smallest / len(split), high / len(split)))
        loudness = loudness * jnp.repeat(draws, shape[axis_at] // shards_of).reshape([-1 if axis == axis_at else 1 for axis in range(len(shape))])
    return loudness


def profile(amount, total, most, skew):
    weights = [(1 << 20) // math.isqrt(rank ** skew) + 1 for rank in range(2, amount + 1)]
    spare, holding = total - most - (amount - 1), [1] * (amount - 1)
    while spare > 0:
        candidates = [i for i in range(amount - 1) if holding[i] < most]
        whole, left = sum([weights[i] for i in candidates]), spare
        for i in candidates:
            addition = min(most - holding[i], max(1, left * weights[i] // whole), spare)
            holding[i] = holding[i] + addition
            spare = spare - addition
    return np.array([most] + holding)


def ragged_sizes(stream_key, number_of, total, limit, slope):
    if number_of == 2:
        one = jax.random.randint(stream_key, (), max(1, total - limit), min(limit, total - 1) + 1)
        return jnp.stack([one, total - one])
    lengths = jnp.asarray(profile(number_of, total, limit, slope), jnp.int32)
    pairs = (number_of - 1) // 2
    source_of, taker = lengths[1:1 + 2 * pairs:2], lengths[2:2 + 2 * pairs:2]
    slack = jnp.minimum(source_of - 1, limit - taker)
    moved = jax.random.randint(jax.random.fold_in(stream_key, 1), (pairs,), 0, 1 << 20) % (slack + 1)
    lengths = lengths.at[1:1 + 2 * pairs:2].set(source_of - moved).at[2:2 + 2 * pairs:2].set(taker + moved)
    return lengths[jax.random.permutation(jax.random.fold_in(stream_key, 2), number_of)]


def bell_draw(key, extent, scale, limit, pieces=(), held_as=jnp.bfloat16):
    array = jax.random.normal(key, extent, jnp.float32) * scale
    if len(pieces) > 0:
        array = levels(key, extent, pieces, -0.22, 0.18) * array
    return jnp.clip(array, min=-limit, max=limit).astype(held_as)


def setup_inputs(seed: int = 0, part: int = 0) -> dict:
    keys = jax.random.split(jax.random.key(seed), 11)
    part_splits = jax.random.split(jax.random.fold_in(keys[10], part), 11)
    pair = bell_draw(part_splits[0], (N, N, C), 1.0, 6.0, ((0, 16),))
    mask = plant((jax.random.randint(part_splits[1], (N,), 0, 8) < 7).astype(jnp.int32), jax.random.fold_in(part_splits[1], 1), 0, 1)
    chain = jnp.searchsorted(jnp.cumsum(ragged_sizes(part_splits[2], 6, N, N // 3, 0)), jnp.arange(N), side="right").astype(jnp.int32)
    tri_proj = bell_draw(keys[3], (C, 4 * C), C ** -0.5, 0.5)
    tri_gate = bell_draw(keys[4], (C, C), C ** -0.5, 0.5)
    tri_out = bell_draw(keys[5], (C, C), C ** -0.5, 0.5)
    att_proj = bell_draw(keys[6], (C, 4 * C), C ** -0.5, 0.5)
    att_bias = draw_att_bias(jax.random.fold_in(keys[10], 71), part)
    same_chain = jnp.clip(jax.random.uniform(keys[8], (H,), jnp.float32, -2.0, 2.0), -2.0, 2.0)
    att_out = bell_draw(keys[9], (C, C), (0.5 / C ** 0.5), 0.26367188)
    return {"pair": pair, "mask": mask, "chain": chain, "tri_proj": tri_proj, "tri_gate": tri_gate, "tri_out": tri_out, "att_proj": att_proj, "att_bias": att_bias, "same_chain": same_chain, "att_out": att_out}


def layer_norm(values):
    centre_mean = lax.optimization_barrier(jnp.mean(values, axis=-1, keepdims=True))
    centred = values - centre_mean
    spread = lax.optimization_barrier(jnp.mean(centred * centred, axis=-1, keepdims=True))
    return centred * lax.rsqrt(spread + 1e-05)

def reference(pair, mask, chain, tri_proj, tri_gate, tri_out, att_proj, att_bias, same_chain, att_out):
    tokens = pair.shape[0]
    width = pair.shape[2]
    head_count = same_chain.shape[0]
    head_size = width // head_count
    scale = head_size ** (-0.5)
    mask_float = mask.astype(jnp.float32)

    def project_row(inputs):
        pair_row, row_mask = inputs
        normed = layer_norm(pair_row.astype(jnp.float32)).astype(jnp.bfloat16)
        projected = jnp.dot(normed, tri_proj, preferred_element_type=jnp.float32)
        weight = (row_mask * mask_float)[:, None]
        left_proj = (weight * jax.nn.sigmoid(projected[:, 2 * width:3 * width]) * projected[:, :width]).astype(jnp.bfloat16)
        right_proj = (weight * jax.nn.sigmoid(projected[:, 3 * width:]) * projected[:, width:2 * width]).astype(jnp.bfloat16)
        out_gate = jax.nn.sigmoid(jnp.dot(normed, tri_gate, preferred_element_type=jnp.float32))
        return (left_proj, right_proj, out_gate)
    left_proj, right_proj, out_gate = lax.map(project_row, (pair, mask_float))
    tri_sum = jnp.einsum('ikc,jkc->ijc', left_proj.astype(jnp.float32), right_proj.astype(jnp.float32), precision=lax.Precision.HIGHEST).astype(jnp.bfloat16)

    def finish_row(inputs):
        pair_row, summed, gate_row = inputs
        tri_norm = layer_norm(summed.astype(jnp.float32)).astype(jnp.bfloat16)
        update = jnp.dot(tri_norm, tri_out, preferred_element_type=jnp.float32)
        mid_pair = (pair_row.astype(jnp.float32) + gate_row * update).astype(jnp.bfloat16)
        mid_norm = layer_norm(mid_pair.astype(jnp.float32)).astype(jnp.bfloat16)
        att_all = jnp.dot(mid_norm, att_proj, preferred_element_type=jnp.float32)
        query = (att_all[:, :width] * scale).astype(jnp.bfloat16)
        key = att_all[:, width:2 * width].astype(jnp.bfloat16)
        value = att_all[:, 2 * width:3 * width].astype(jnp.bfloat16)
        att_gate = jax.nn.sigmoid(att_all[:, 3 * width:])
        pair_bias = jnp.dot(mid_norm, att_bias.astype(jnp.float32), preferred_element_type=jnp.float32).astype(jnp.bfloat16)
        return (mid_pair, query, key, value, att_gate, pair_bias)
    mid_pair, query, key, value, att_gate, pair_bias = lax.map(finish_row, (pair, tri_sum, out_gate))
    same = (chain[:, None] == chain[None, :]).astype(jnp.float32)
    logit_bias = jnp.transpose(pair_bias.astype(jnp.float32), (2, 0, 1)) + same_chain[:, None, None] * same[None, :, :]
    logit_bias = logit_bias + 10000.0 * (mask_float - 1.0)[None, None, :]

    def attend_row(inputs):
        query_row, key_row, value_row, gate_row, mid_row = inputs
        query_heads = query_row.reshape(tokens, head_count, head_size).astype(jnp.float32)
        key_heads = key_row.reshape(tokens, head_count, head_size).astype(jnp.float32)
        value_heads = value_row.reshape(tokens, head_count, head_size).astype(jnp.float32)
        scores = jnp.einsum('jhd,khd->hjk', query_heads, key_heads, precision=lax.Precision.HIGHEST) + logit_bias
        row_max = lax.optimization_barrier(jnp.max(scores, axis=2, keepdims=True))
        exp_scores = jnp.exp(scores - row_max)
        weight = (exp_scores / lax.optimization_barrier(jnp.sum(exp_scores, axis=2, keepdims=True))).astype(jnp.bfloat16)
        mixed_heads = jnp.einsum('hjk,khd->jhd', weight.astype(jnp.float32), value_heads, precision=lax.Precision.HIGHEST).reshape(tokens, width)
        gated = (gate_row * mixed_heads).astype(jnp.bfloat16)
        return (mid_row.astype(jnp.float32) + jnp.dot(gated, att_out, preferred_element_type=jnp.float32)).astype(jnp.bfloat16)
    return lax.map(attend_row, (query, key, value, att_gate, mid_pair))
```

```python
import jax
import jax.numpy as jnp
from jax import lax
from jax.experimental import pallas as pl
from jax.experimental.pallas import tpu as pltpu
from jax.sharding import PartitionSpec as P

F32 = jnp.float32
BF16 = jnp.bfloat16
NT = (((1,), (1,)), ((), ()))
TN = (((0,), (0,)), ((), ()))


def layer_norm(values):
    centre_mean = jnp.mean(values, axis=-1, keepdims=True)
    centred = values - centre_mean
    spread = jnp.mean(centred * centred, axis=-1, keepdims=True)
    return centred * lax.rsqrt(spread + 1e-05)


def chain_logits(bias_block, same_chain, chain_rows, chain, mask_float):
    same = (chain_rows[:, None] == chain[None, :]).astype(jnp.float32)
    logit_bias = bias_block.astype(jnp.float32) + same_chain[:, None, None] * same[None, :, :]
    return logit_bias + 10000.0 * (mask_float - 1.0)[None, None, :]


def attend(query, att_gate, key, value, logit_bias, head_count, head_size):
    block_len = query.shape[1]
    tokens = key.shape[1]
    width = head_count * head_size

    def one_row(inputs):
        query_row, key_row, value_row, gate_row = inputs
        query_heads = query_row.reshape(block_len, head_count, head_size)
        key_heads = key_row.reshape(tokens, head_count, head_size)
        value_heads = value_row.reshape(tokens, head_count, head_size)
        scores = (
            jnp.einsum("jhd,khd->hjk", query_heads, key_heads, preferred_element_type=jnp.float32)
            + logit_bias
        )
        row_max = jnp.max(scores, axis=2, keepdims=True)
        exp_scores = jnp.exp(scores - row_max)
        weight = (exp_scores / jnp.sum(exp_scores, axis=2, keepdims=True)).astype(jnp.bfloat16)
        mixed_heads = jnp.einsum(
            "hjk,khd->jhd", weight, value_heads, preferred_element_type=jnp.float32
        )
        return (gate_row * mixed_heads.reshape(block_len, width)).astype(jnp.bfloat16)

    return lax.map(one_row, (query, key, value, att_gate))


def per_device_general(
    pair, mask, chain, tri_proj, tri_gate, tri_out, att_proj, att_bias, same_chain, att_out
):
    local_rows, tokens, width = pair.shape
    head_count = same_chain.shape[0]
    head_size = width // head_count
    scale = head_size ** (-0.5)
    part_count = lax.axis_size("row")
    share_width = width // part_count
    first_row = lax.axis_index("row") * local_rows
    mask_float = mask.astype(jnp.float32)
    row_mask = lax.dynamic_slice_in_dim(mask_float, first_row, local_rows)

    def project_row(inputs):
        pair_row, mask_value = inputs
        normed = layer_norm(pair_row.astype(jnp.float32)).astype(jnp.bfloat16)
        projected = jnp.dot(normed, tri_proj, preferred_element_type=jnp.float32)
        weight = (mask_value * mask_float)[:, None]
        left_proj = (
            weight * jax.nn.sigmoid(projected[:, 2 * width : 3 * width]) * projected[:, :width]
        ).astype(jnp.bfloat16)
        right_proj = (
            weight * jax.nn.sigmoid(projected[:, 3 * width :]) * projected[:, width : 2 * width]
        ).astype(jnp.bfloat16)
        out_gate = jax.nn.sigmoid(jnp.dot(normed, tri_gate, preferred_element_type=jnp.float32))
        return (left_proj, right_proj, out_gate)

    left_proj, right_proj, out_gate = lax.map(project_row, (pair, row_mask))
    left_lay = jnp.transpose(left_proj, (2, 0, 1)).reshape(
        part_count, share_width, local_rows, tokens
    )
    right_lay = jnp.transpose(right_proj, (2, 0, 1)).reshape(
        part_count, share_width, local_rows, tokens
    )
    got_left, got_right = (
        lax.all_to_all(left_lay, "row", split_axis=0, concat_axis=2, tiled=True),
        lax.all_to_all(right_lay, "row", split_axis=0, concat_axis=2, tiled=True),
    )
    product = jnp.einsum(
        "cik,cjk->cij", got_left[0], got_right[0], preferred_element_type=jnp.float32
    )
    returned = lax.all_to_all(
        product.astype(jnp.bfloat16)[None], "row", split_axis=2, concat_axis=0, tiled=True
    )
    tri_sum = jnp.transpose(returned.reshape(width, local_rows, tokens), (1, 2, 0))

    def finish_row(inputs):
        pair_row, summed, gate_row = inputs
        tri_norm = layer_norm(summed.astype(jnp.float32)).astype(jnp.bfloat16)
        update = jnp.dot(tri_norm, tri_out, preferred_element_type=jnp.float32)
        mid_pair = (pair_row.astype(jnp.float32) + gate_row * update).astype(jnp.bfloat16)
        mid_norm = layer_norm(mid_pair.astype(jnp.float32)).astype(jnp.bfloat16)
        att_all = jnp.dot(mid_norm, att_proj, preferred_element_type=jnp.float32)
        query = (att_all[:, :width] * scale).astype(jnp.bfloat16)
        key = att_all[:, width : 2 * width].astype(jnp.bfloat16)
        value = att_all[:, 2 * width : 3 * width].astype(jnp.bfloat16)
        att_gate = jax.nn.sigmoid(att_all[:, 3 * width :])
        pair_bias = jnp.dot(mid_norm, att_bias, preferred_element_type=jnp.float32).astype(
            jnp.bfloat16
        )
        return (mid_pair, query, key, value, att_gate, pair_bias)

    mid_pair, query, key, value, att_gate, pair_bias = lax.map(
        finish_row, (pair, tri_sum, out_gate)
    )
    bias_lay = jnp.transpose(pair_bias, (2, 0, 1))
    full_bias = lax.all_gather(bias_lay, "row", axis=1, tiled=True)
    logit_bias = chain_logits(full_bias, same_chain, chain, chain, mask_float)
    gated = attend(query, att_gate, key, value, logit_bias, head_count, head_size)
    projected_out = jnp.dot(gated.reshape(-1, width), att_out, preferred_element_type=jnp.float32)
    return (mid_pair.astype(jnp.float32) + projected_out.reshape(local_rows, tokens, width)).astype(
        jnp.bfloat16
    )


ROWS, TOKENS, WIDTH, PARTS, HEADS = 10, 160, 128, 16, 4
SHARE = WIDTH // PARTS
TAIL = TOKENS - 128


def dot(left, right, dims):
    return lax.dot_general(left, right, dims, preferred_element_type=F32)


def norm(values, axis):
    centred = values - jnp.mean(values, axis=axis, keepdims=True)
    spread = jnp.mean(centred * centred, axis=axis, keepdims=True)
    return (centred * lax.rsqrt(spread + 1e-05)).astype(BF16)


def pad_lanes(values):
    return jnp.concatenate(
        [values, jnp.zeros((values.shape[0], 128 - values.shape[1]), values.dtype)], axis=1
    )


def fused_kernel(
    mask_s,
    same_s,
    pair,
    mask_v,
    chain_v,
    tri_proj,
    tri_gate,
    tri_out,
    att_proj,
    bias_t,
    att_out,
    out,
    proj_t,
    normed,
    tails,
    send1,
    recv1,
    main_f,
    tail_f,
    sum_m,
    sum_t,
    send2,
    recv2,
    recv2_f,
    summed,
    gate,
    mid,
    mid_norm,
    bias_rows,
    send3,
    recv3,
    bias_m,
    bias_tl,
    logit,
    query,
    key,
    value,
    att_gate,
    sends,
    recvs,
):
    me = lax.axis_index("row")

    def other(step):
        return lax.rem(me + step, PARTS)

    barrier = pltpu.get_barrier_semaphore()

    @pl.loop(1, PARTS)
    def _(step):
        pl.semaphore_signal(
            barrier, inc=1, device_id={"row": other(step)}, device_id_type=pl.DeviceIdType.MESH
        )

    def copy_to(phase, source, landing, part):
        return pltpu.make_async_remote_copy(
            src_ref=source,
            dst_ref=landing.at[me],
            send_sem=sends.at[phase, part],
            recv_sem=recvs.at[phase, me],
            device_id={"row": part},
            device_id_type=pl.DeviceIdType.MESH,
        )

    def arrived(phase, landing, source):
        return pltpu.make_async_remote_copy(
            src_ref=landing.at[source],
            dst_ref=landing.at[source],
            send_sem=sends.at[phase, source],
            recv_sem=recvs.at[phase, source],
            device_id={"row": source},
            device_id_type=pl.DeviceIdType.MESH,
        )

    turned = tri_proj[...].astype(F32).T
    pieces = []
    for half in range(2):
        for part in range(PARTS):
            for side in range(2):
                at = half * 2 * WIDTH + side * WIDTH + part * SHARE
                pieces.append(turned[at : at + SHARE])
    proj_t[...] = jnp.concatenate(pieces, axis=0).astype(BF16)
    mask_row = mask_v[...].astype(F32)

    @pl.loop(0, ROWS)
    def _(i):
        row = norm(pair[i].astype(F32), 1)
        normed[i] = row
        projected = dot(proj_t[...], row, NT)
        weight = mask_row * mask_s[me * ROWS + i].astype(F32)
        both = weight * jax.nn.sigmoid(projected[2 * WIDTH :]) * projected[: 2 * WIDTH]
        send1[:, i] = both[:, :128].astype(BF16).reshape(PARTS, 16, 128)
        tails[i] = both[:, 128:]

    for tile in range(3):
        parts = [tails[i] for i in range(4 * tile, min(4 * tile + 4, ROWS))]
        packed = jnp.concatenate(parts, axis=1)
        if len(parts) < 4:
            packed = pad_lanes(packed)
        send1[:, ROWS + tile] = packed.astype(BF16).reshape(PARTS, 16, 128)

    pl.semaphore_wait(barrier, PARTS - 1)

    @pl.loop(1, PARTS)
    def _(step):
        part = other(step)
        copy_to(0, send1.at[part], recv1, part).start()

    recv1[me] = send1[me]

    @pl.loop(0, ROWS)
    def _(i):
        gate[i] = jax.nn.sigmoid(jnp.dot(normed[i], tri_gate[...], preferred_element_type=F32))

    @pl.loop(0, PARTS)
    def _(step):
        source = other(step)

        @pl.when(step > 0)
        def _():
            arrived(0, recv1, source).wait_recv()

        for i in range(ROWS):
            at = pl.multiple_of((source * ROWS + i) * 16, 16)
            main_f[pl.ds(at, 16), :] = recv1[source, i].astype(F32)
            lane = TAIL * (i % 4)
            tail = recv1[source, ROWS + i // 4].astype(F32)[:, lane : lane + TAIL]
            tail_f[pl.ds(at, 16), 0:TAIL] = tail

    for c in range(SHARE):
        at_l, at_r = pl.ds(c, TOKENS, stride=16), pl.ds(SHARE + c, TOKENS, stride=16)
        main = dot(main_f[at_l, :].astype(BF16), main_f[at_r, :].astype(BF16), NT)
        tail = dot(
            tail_f[at_l, :][:, :TAIL].astype(BF16), tail_f[at_r, :][:, :TAIL].astype(BF16), NT
        )
        total = main + tail
        sum_m[pl.ds(c, TOKENS, stride=SHARE), :] = total[:, :128]
        sum_t[pl.ds(c, TOKENS, stride=SHARE), :] = pad_lanes(total[:, 128:])

    @pl.loop(0, PARTS)
    def _(step):
        part = other(step)
        at = pl.multiple_of(part * ROWS * SHARE, ROWS * SHARE)
        send2[part, 0:80] = sum_m[pl.ds(at, 80), :].astype(BF16)
        rest = sum_t[pl.ds(at, 80), :][:, :TAIL]
        packed = jnp.concatenate([rest[16 * t : 16 * t + 16] for t in range(4)], axis=1)
        send2[part, 80:96] = packed.astype(BF16)
        send2[part, 96:112] = pad_lanes(rest[64:80]).astype(BF16)

        @pl.when(step > 0)
        def _():
            copy_to(1, send2.at[part], recv2, part).start()

    recv2[me] = send2[me]

    @pl.loop(0, PARTS)
    def _(step):
        source = other(step)

        @pl.when(step > 0)
        def _():
            arrived(1, recv2, source).wait_recv()

        recv2_f[source] = recv2[source].astype(F32)

    for i in range(ROWS):
        summed[i, :, 0:128] = recv2_f[:, SHARE * i : SHARE * i + SHARE, :].reshape(WIDTH, 128)
        row = 80 + SHARE * (i % 2) + (16 if i >= 8 else 0)
        lane = TAIL * ((i // 2) % 4)
        rest = recv2_f[:, row : row + SHARE, :].reshape(WIDTH, 128)
        summed[i, :, 128:TOKENS] = rest[:, lane : lane + TAIL]

    @pl.loop(0, ROWS // 2)
    def _(pair_at):
        biases = []
        for half in range(2):
            i = pair_at * 2 + half
            tri_norm = norm(summed[i], 0)
            update = dot(tri_norm, tri_out[...], TN)
            mid_row = (pair[i].astype(F32) + gate[i] * update).astype(BF16)
            mid[i] = mid_row
            mid_n = norm(mid_row.astype(F32), 1)
            mid_norm[i] = mid_n
            bias = dot(bias_t[...], mid_n, NT)
            biases.append(bias[0:8] + bias[8:16])
        joined = jnp.concatenate([biases[0][0:HEADS], biases[1][0:HEADS]], axis=0)
        bias_rows[pl.ds(pl.multiple_of(pair_at * 8, 8), 8), :] = joined

    send3[0:32] = bias_rows[0:32, 0:128].astype(BF16)
    send3[32:48] = jnp.concatenate(
        [bias_rows[32:40, 0:128], jnp.zeros((8, 128), F32)], axis=0
    ).astype(BF16)
    last = jnp.concatenate([bias_rows[32:40, 128:TOKENS], jnp.zeros((8, TAIL), F32)], axis=0)
    send3[48:64] = pad_lanes(
        jnp.concatenate(
            [bias_rows[0:16, 128:TOKENS], bias_rows[16:32, 128:TOKENS], last], axis=1
        )
    ).astype(BF16)

    @pl.loop(1, PARTS)
    def _(step):
        part = other(step)
        copy_to(2, send3, recv3, part).start()

    recv3[me] = send3[...]

    query_t = att_proj[:, 0:WIDTH].astype(F32).T.astype(BF16)
    channel = lax.broadcasted_iota(jnp.int32, (WIDTH, HEADS * TOKENS), 0) // (WIDTH // HEADS)
    lane = lax.broadcasted_iota(jnp.int32, (WIDTH, HEADS * TOKENS), 1)
    block = (lane >= channel * TOKENS) & (lane < channel * TOKENS + TOKENS)
    scale = (WIDTH // HEADS) ** (-0.5)

    @pl.loop(0, ROWS)
    def _(i):
        mid_n = mid_norm[i]
        rest = jnp.dot(mid_n, att_proj[:, WIDTH:], preferred_element_type=F32)
        key[i] = rest[:, 0:WIDTH].astype(BF16)
        value[i] = rest[:, WIDTH : 2 * WIDTH].astype(BF16)
        att_gate[i] = jax.nn.sigmoid(rest[:, 2 * WIDTH :])
        wide = dot(query_t, jnp.concatenate([mid_n] * HEADS, axis=0), NT)
        query[i] = jnp.where(block, wide * scale, 0.0).astype(BF16)

    ids = lax.broadcasted_iota(jnp.int32, (16, TOKENS), 0)
    one_hot = jnp.where(ids == chain_v[...], 1.0, 0.0).astype(BF16)
    same = dot(one_hot, one_hot, TN)
    absent = 10000.0 * (mask_row - 1.0)

    @pl.loop(0, PARTS)
    def _(step):
        source = other(step)

        @pl.when(step > 0)
        def _():
            arrived(2, recv3, source).wait_recv()

        at = pl.multiple_of(source * 40, 8)
        got = recv3[source].astype(F32)
        bias_m[pl.ds(at, 40), :] = got[0:40]
        for t in range(3):
            size = 16 if t < 2 else 8
            bias_tl[pl.ds(pl.multiple_of(at + 16 * t, 8), size), 0:TAIL] = got[
                48 : 48 + size, TAIL * t : TAIL * t + TAIL
            ]

    mains, rests = [], []
    for h in range(HEADS):
        extra = same_s[h] * same
        every = pl.ds(h, TOKENS, stride=HEADS)
        mains.append(bias_m[every, :] + extra[:, 0:128] + absent[:, 0:128])
        rest = bias_tl[every, :][:, :TAIL] + extra[:, 128:] + absent[:, 128:]
        rests.append(pad_lanes(rest))
    logit[0:128, :] = jnp.concatenate(mains, axis=0).T
    logit[128:TOKENS, :] = jnp.concatenate(rests, axis=0).T[0:TAIL]

    head_of = lax.broadcasted_iota(jnp.int32, (TOKENS, WIDTH), 1) // (WIDTH // HEADS)

    @pl.loop(0, ROWS)
    def _(i):
        scores = jnp.dot(key[i], query[i], preferred_element_type=F32) + logit[...]
        top = jnp.max(scores, axis=0, keepdims=True)
        exps = jnp.exp(scores - top)
        weight = (exps * (1.0 / jnp.sum(exps, axis=0, keepdims=True))).astype(BF16)
        mixes = dot(weight, value[i], TN)
        mixed = mixes[0:TOKENS]
        for h in range(1, HEADS):
            mixed = jnp.where(head_of == h, mixes[h * TOKENS : (h + 1) * TOKENS], mixed)
        gated = (att_gate[i] * mixed).astype(BF16)
        added = jnp.dot(gated, att_out[...], preferred_element_type=F32)
        out[i] = (mid[i].astype(F32) + added).astype(BF16)

    @pl.loop(1, PARTS)
    def _(step):
        part = other(step)
        copy_to(0, send1.at[part], recv1, part).wait_send()
        copy_to(1, send2.at[part], recv2, part).wait_send()
        copy_to(2, send3, recv3, part).wait_send()


def per_device_fused(
    pair, mask, chain, tri_proj, tri_gate, tri_out, att_proj, att_bias, same_chain, att_out
):
    turned = att_bias.T
    high = turned.astype(BF16)
    low = (turned - high.astype(F32)).astype(BF16)
    zeros = jnp.zeros((HEADS, WIDTH), BF16)
    bias_t = jnp.concatenate([high, zeros, low, zeros], axis=0)
    smem = pl.BlockSpec(memory_space=pltpu.SMEM)
    vmem = pl.BlockSpec(memory_space=pltpu.VMEM)
    all_rows = (ROWS, TOKENS, WIDTH)
    return pl.pallas_call(
        fused_kernel,
        out_shape=jax.ShapeDtypeStruct(all_rows, BF16),
        in_specs=[smem, smem] + [vmem] * 9,
        out_specs=vmem,
        scratch_shapes=[
            pltpu.VMEM((4 * WIDTH, WIDTH), BF16),
            pltpu.VMEM(all_rows, BF16),
            pltpu.VMEM((ROWS, 2 * WIDTH, TAIL), F32),
            pltpu.VMEM((PARTS, 13, 16, 128), BF16),
            pltpu.VMEM((PARTS, 13, 16, 128), BF16),
            pltpu.VMEM((TOKENS * 16, 128), F32),
            pltpu.VMEM((TOKENS * 16, 128), F32),
            pltpu.VMEM((TOKENS * SHARE, 128), F32),
            pltpu.VMEM((TOKENS * SHARE, 128), F32),
            pltpu.VMEM((PARTS, 112, 128), BF16),
            pltpu.VMEM((PARTS, 112, 128), BF16),
            pltpu.VMEM((PARTS, 112, 128), F32),
            pltpu.VMEM((ROWS, WIDTH, TOKENS), F32),
            pltpu.VMEM(all_rows, F32),
            pltpu.VMEM(all_rows, BF16),
            pltpu.VMEM(all_rows, BF16),
            pltpu.VMEM((40, TOKENS), F32),
            pltpu.VMEM((64, 128), BF16),
            pltpu.VMEM((PARTS, 64, 128), BF16),
            pltpu.VMEM((TOKENS * HEADS, 128), F32),
            pltpu.VMEM((TOKENS * HEADS, 128), F32),
            pltpu.VMEM((TOKENS, HEADS * TOKENS), F32),
            pltpu.VMEM((ROWS, WIDTH, HEADS * TOKENS), BF16),
            pltpu.VMEM(all_rows, BF16),
            pltpu.VMEM(all_rows, BF16),
            pltpu.VMEM(all_rows, F32),
            pltpu.SemaphoreType.DMA((3, PARTS)),
            pltpu.SemaphoreType.DMA((3, PARTS)),
        ],
        compiler_params=pltpu.CompilerParams(
            collective_id=0, has_side_effects=True, vmem_limit_bytes=40 * 1024 * 1024
        ),
    )(
        mask,
        same_chain,
        pair,
        mask.reshape(1, TOKENS),
        chain.reshape(1, TOKENS),
        tri_proj,
        tri_gate,
        tri_out,
        att_proj,
        bias_t,
        att_out,
    )


def per_device(pair, *others):
    fits = pair.shape == (ROWS, TOKENS, WIDTH) and lax.axis_size("row") == PARTS
    return (per_device_fused if fits else per_device_general)(pair, *others)


def solution(mesh):
    return jax.shard_map(
        per_device,
        mesh=mesh,
        in_specs=(
            P(("groups", "row"), None, None),
            P("groups"),
            P("groups"),
            P(),
            P(),
            P(),
            P(),
            P(),
            P(),
            P(),
        ),
        out_specs=P(("groups", "row"), None, None),
        check_vma=False,
    )
```

```python
import jax
import jax.numpy as jnp
from jax import lax
from jax.experimental import pallas as pl
from jax.experimental.pallas import tpu as pltpu
from jax.sharding import PartitionSpec as P

F32 = jnp.float32
BF16 = jnp.bfloat16
NT = (((1,), (1,)), ((), ()))
TN = (((0,), (0,)), ((), ()))


def layer_norm(values):
    centre_mean = jnp.mean(values, axis=-1, keepdims=True)
    centred = values - centre_mean
    spread = jnp.mean(centred * centred, axis=-1, keepdims=True)
    return centred * lax.rsqrt(spread + 1e-05)


def chain_logits(bias_block, same_chain, chain_rows, chain, mask_float):
    same = (chain_rows[:, None] == chain[None, :]).astype(jnp.float32)
    logit_bias = bias_block.astype(jnp.float32) + same_chain[:, None, None] * same[None, :, :]
    return logit_bias + 10000.0 * (mask_float - 1.0)[None, None, :]


def attend(query, att_gate, key, value, logit_bias, head_count, head_size):
    block_len = query.shape[1]
    tokens = key.shape[1]
    width = head_count * head_size

    def one_row(inputs):
        query_row, key_row, value_row, gate_row = inputs
        query_heads = query_row.reshape(block_len, head_count, head_size)
        key_heads = key_row.reshape(tokens, head_count, head_size)
        value_heads = value_row.reshape(tokens, head_count, head_size)
        scores = (
            jnp.einsum("jhd,khd->hjk", query_heads, key_heads, preferred_element_type=jnp.float32)
            + logit_bias
        )
        row_max = jnp.max(scores, axis=2, keepdims=True)
        exp_scores = jnp.exp(scores - row_max)
        weight = (exp_scores / jnp.sum(exp_scores, axis=2, keepdims=True)).astype(jnp.bfloat16)
        mixed_heads = jnp.einsum(
            "hjk,khd->jhd", weight, value_heads, preferred_element_type=jnp.float32
        )
        return (gate_row * mixed_heads.reshape(block_len, width)).astype(jnp.bfloat16)

    return lax.map(one_row, (query, key, value, att_gate))


def per_device_general(
    pair, mask, chain, tri_proj, tri_gate, tri_out, att_proj, att_bias, same_chain, att_out
):
    local_rows, tokens, width = pair.shape
    head_count = same_chain.shape[0]
    head_size = width // head_count
    scale = head_size ** (-0.5)
    part_count = lax.axis_size("row")
    share_width = width // part_count
    first_row = lax.axis_index("row") * local_rows
    mask_float = mask.astype(jnp.float32)
    row_mask = lax.dynamic_slice_in_dim(mask_float, first_row, local_rows)

    def project_row(inputs):
        pair_row, mask_value = inputs
        normed = layer_norm(pair_row.astype(jnp.float32)).astype(jnp.bfloat16)
        projected = jnp.dot(normed, tri_proj, preferred_element_type=jnp.float32)
        weight = (mask_value * mask_float)[:, None]
        left_proj = (
            weight * jax.nn.sigmoid(projected[:, 2 * width : 3 * width]) * projected[:, :width]
        ).astype(jnp.bfloat16)
        right_proj = (
            weight * jax.nn.sigmoid(projected[:, 3 * width :]) * projected[:, width : 2 * width]
        ).astype(jnp.bfloat16)
        out_gate = jax.nn.sigmoid(jnp.dot(normed, tri_gate, preferred_element_type=jnp.float32))
        return (left_proj, right_proj, out_gate)

    left_proj, right_proj, out_gate = lax.map(project_row, (pair, row_mask))
    left_lay = jnp.transpose(left_proj, (2, 0, 1)).reshape(
        part_count, share_width, local_rows, tokens
    )
    right_lay = jnp.transpose(right_proj, (2, 0, 1)).reshape(
        part_count, share_width, local_rows, tokens
    )
    got_left, got_right = (
        lax.all_to_all(left_lay, "row", split_axis=0, concat_axis=2, tiled=True),
        lax.all_to_all(right_lay, "row", split_axis=0, concat_axis=2, tiled=True),
    )
    product = jnp.einsum(
        "cik,cjk->cij", got_left[0], got_right[0], preferred_element_type=jnp.float32
    )
    returned = lax.all_to_all(
        product.astype(jnp.bfloat16)[None], "row", split_axis=2, concat_axis=0, tiled=True
    )
    tri_sum = jnp.transpose(returned.reshape(width, local_rows, tokens), (1, 2, 0))

    def finish_row(inputs):
        pair_row, summed, gate_row = inputs
        tri_norm = layer_norm(summed.astype(jnp.float32)).astype(jnp.bfloat16)
        update = jnp.dot(tri_norm, tri_out, preferred_element_type=jnp.float32)
        mid_pair = (pair_row.astype(jnp.float32) + gate_row * update).astype(jnp.bfloat16)
        mid_norm = layer_norm(mid_pair.astype(jnp.float32)).astype(jnp.bfloat16)
        att_all = jnp.dot(mid_norm, att_proj, preferred_element_type=jnp.float32)
        query = (att_all[:, :width] * scale).astype(jnp.bfloat16)
        key = att_all[:, width : 2 * width].astype(jnp.bfloat16)
        value = att_all[:, 2 * width : 3 * width].astype(jnp.bfloat16)
        att_gate = jax.nn.sigmoid(att_all[:, 3 * width :])
        pair_bias = jnp.dot(mid_norm, att_bias, preferred_element_type=jnp.float32).astype(
            jnp.bfloat16
        )
        return (mid_pair, query, key, value, att_gate, pair_bias)

    mid_pair, query, key, value, att_gate, pair_bias = lax.map(
        finish_row, (pair, tri_sum, out_gate)
    )
    bias_lay = jnp.transpose(pair_bias, (2, 0, 1))
    full_bias = lax.all_gather(bias_lay, "row", axis=1, tiled=True)
    logit_bias = chain_logits(full_bias, same_chain, chain, chain, mask_float)
    gated = attend(query, att_gate, key, value, logit_bias, head_count, head_size)
    projected_out = jnp.dot(gated.reshape(-1, width), att_out, preferred_element_type=jnp.float32)
    return (mid_pair.astype(jnp.float32) + projected_out.reshape(local_rows, tokens, width)).astype(
        jnp.bfloat16
    )


ROWS, TOKENS, WIDTH, PARTS, HEADS = 10, 160, 128, 16, 4
SHARE = WIDTH // PARTS
TAIL = TOKENS - 128


def dot(left, right, dims):
    return lax.dot_general(left, right, dims, preferred_element_type=F32)


def norm(values, axis):
    centred = values - jnp.mean(values, axis=axis, keepdims=True)
    spread = jnp.mean(centred * centred, axis=axis, keepdims=True)
    return (centred * lax.rsqrt(spread + 1e-05)).astype(BF16)


def pad_lanes(values):
    return jnp.concatenate(
        [values, jnp.zeros((values.shape[0], 128 - values.shape[1]), values.dtype)], axis=1
    )


def fused_kernel(
    *refs,
):
    outside, (out, *inside, loads) = refs[:10], refs[10:]
    held, scratch = inside[:10], inside[10:]
    fetches = [
        pltpu.make_async_copy(source, target, loads.at[k])
        for k, (source, target) in enumerate(zip(outside, held))
    ]
    for fetch in fetches:
        fetch.start()
    fused_body(fetches, out, *held, *scratch)


def fused_body(
    fetches,
    out,
    pair,
    tri_proj,
    mask_v,
    tri_gate,
    tri_out,
    bias_t,
    att_proj,
    chain_v,
    same_v,
    att_out,
    proj_t,
    normed,
    tails,
    send1,
    recv1,
    main_f,
    tail_f,
    sum_m,
    sum_t,
    send2,
    recv2,
    recv2_f,
    summed,
    gate,
    mid,
    mid_norm,
    bias_rows,
    send3,
    recv3,
    bias_m,
    bias_tl,
    logit,
    query,
    key,
    value,
    att_gate,
    sends,
    recvs,
):
    me = lax.axis_index("row")

    def other(step):
        return lax.rem(me + step, PARTS)

    barrier = pltpu.get_barrier_semaphore()

    @pl.loop(1, PARTS)
    def _(step):
        pl.semaphore_signal(
            barrier, inc=1, device_id={"row": other(step)}, device_id_type=pl.DeviceIdType.MESH
        )

    def copy_to(phase, source, landing, part):
        return pltpu.make_async_remote_copy(
            src_ref=source,
            dst_ref=landing.at[me],
            send_sem=sends.at[phase, part],
            recv_sem=recvs.at[phase, me],
            device_id={"row": part},
            device_id_type=pl.DeviceIdType.MESH,
        )

    def arrived(phase, landing, source):
        return pltpu.make_async_remote_copy(
            src_ref=landing.at[source],
            dst_ref=landing.at[source],
            send_sem=sends.at[phase, source],
            recv_sem=recvs.at[phase, source],
            device_id={"row": source},
            device_id_type=pl.DeviceIdType.MESH,
        )

    for fetch in fetches[:3]:
        fetch.wait()

    turned = tri_proj[...].astype(F32).T
    pieces = []
    for half in range(2):
        for part in range(PARTS):
            for side in range(2):
                at = half * 2 * WIDTH + side * WIDTH + part * SHARE
                pieces.append(turned[at : at + SHARE])
    proj_t[...] = jnp.concatenate(pieces, axis=0).astype(BF16)
    mask_row = mask_v[...].astype(F32)
    token = lax.broadcasted_iota(jnp.int32, (1, TOKENS), 1)

    @pl.loop(0, ROWS)
    def _(i):
        row = norm(pair[i].astype(F32), 1)
        normed[i] = row
        projected = dot(proj_t[...], row, NT)
        mine = jnp.where(token == me * ROWS + i, mask_row, 0.0)
        weight = mask_row * jnp.sum(mine, axis=1, keepdims=True)
        both = weight * jax.nn.sigmoid(projected[2 * WIDTH :]) * projected[: 2 * WIDTH]
        send1[:, i] = both[:, :128].astype(BF16).reshape(PARTS, 16, 128)
        tails[i] = both[:, 128:]

    for tile in range(3):
        parts = [tails[i] for i in range(4 * tile, min(4 * tile + 4, ROWS))]
        packed = jnp.concatenate(parts, axis=1)
        if len(parts) < 4:
            packed = pad_lanes(packed)
        send1[:, ROWS + tile] = packed.astype(BF16).reshape(PARTS, 16, 128)

    pl.semaphore_wait(barrier, PARTS - 1)

    @pl.loop(1, PARTS)
    def _(step):
        part = other(step)
        copy_to(0, send1.at[part], recv1, part).start()

    recv1[me] = send1[me]
    for fetch in fetches[3:]:
        fetch.wait()

    @pl.loop(0, ROWS)
    def _(i):
        gate[i] = jax.nn.sigmoid(jnp.dot(normed[i], tri_gate[...], preferred_element_type=F32))

    @pl.loop(0, PARTS)
    def _(step):
        source = other(step)

        @pl.when(step > 0)
        def _():
            arrived(0, recv1, source).wait_recv()

        for i in range(ROWS):
            at = pl.multiple_of((source * ROWS + i) * 16, 16)
            main_f[pl.ds(at, 16), :] = recv1[source, i].astype(F32)
            lane = TAIL * (i % 4)
            tail = recv1[source, ROWS + i // 4].astype(F32)[:, lane : lane + TAIL]
            tail_f[pl.ds(at, 16), 0:TAIL] = tail

    for c in range(SHARE):
        at_l, at_r = pl.ds(c, TOKENS, stride=16), pl.ds(SHARE + c, TOKENS, stride=16)
        main = dot(main_f[at_l, :].astype(BF16), main_f[at_r, :].astype(BF16), NT)
        tail = dot(
            tail_f[at_l, :][:, :TAIL].astype(BF16), tail_f[at_r, :][:, :TAIL].astype(BF16), NT
        )
        total = main + tail
        sum_m[pl.ds(c, TOKENS, stride=SHARE), :] = total[:, :128]
        sum_t[pl.ds(c, TOKENS, stride=SHARE), :] = pad_lanes(total[:, 128:])

    @pl.loop(0, PARTS)
    def _(step):
        part = other(step)
        at = pl.multiple_of(part * ROWS * SHARE, ROWS * SHARE)
        send2[part, 0:80] = sum_m[pl.ds(at, 80), :].astype(BF16)
        rest = sum_t[pl.ds(at, 80), :][:, :TAIL]
        packed = jnp.concatenate([rest[16 * t : 16 * t + 16] for t in range(4)], axis=1)
        send2[part, 80:96] = packed.astype(BF16)
        send2[part, 96:112] = pad_lanes(rest[64:80]).astype(BF16)

        @pl.when(step > 0)
        def _():
            copy_to(1, send2.at[part], recv2, part).start()

    recv2[me] = send2[me]

    @pl.loop(0, PARTS)
    def _(step):
        source = other(step)

        @pl.when(step > 0)
        def _():
            arrived(1, recv2, source).wait_recv()

        recv2_f[source] = recv2[source].astype(F32)

    for i in range(ROWS):
        summed[i, :, 0:128] = recv2_f[:, SHARE * i : SHARE * i + SHARE, :].reshape(WIDTH, 128)
        row = 80 + SHARE * (i % 2) + (16 if i >= 8 else 0)
        lane = TAIL * ((i // 2) % 4)
        rest = recv2_f[:, row : row + SHARE, :].reshape(WIDTH, 128)
        summed[i, :, 128:TOKENS] = rest[:, lane : lane + TAIL]

    @pl.loop(0, ROWS // 2)
    def _(pair_at):
        biases = []
        for half in range(2):
            i = pair_at * 2 + half
            tri_norm = norm(summed[i], 0)
            update = dot(tri_norm, tri_out[...], TN)
            mid_row = (pair[i].astype(F32) + gate[i] * update).astype(BF16)
            mid[i] = mid_row
            mid_n = norm(mid_row.astype(F32), 1)
            mid_norm[i] = mid_n
            bias = dot(bias_t[...], mid_n, NT)
            biases.append(bias[0:8] + bias[8:16])
        joined = jnp.concatenate([biases[0][0:HEADS], biases[1][0:HEADS]], axis=0)
        bias_rows[pl.ds(pl.multiple_of(pair_at * 8, 8), 8), :] = joined

    send3[0:32] = bias_rows[0:32, 0:128].astype(BF16)
    send3[32:48] = jnp.concatenate(
        [bias_rows[32:40, 0:128], jnp.zeros((8, 128), F32)], axis=0
    ).astype(BF16)
    last = jnp.concatenate([bias_rows[32:40, 128:TOKENS], jnp.zeros((8, TAIL), F32)], axis=0)
    send3[48:64] = pad_lanes(
        jnp.concatenate(
            [bias_rows[0:16, 128:TOKENS], bias_rows[16:32, 128:TOKENS], last], axis=1
        )
    ).astype(BF16)

    @pl.loop(1, PARTS)
    def _(step):
        part = other(step)
        copy_to(2, send3, recv3, part).start()

    recv3[me] = send3[...]

    query_t = att_proj[:, 0:WIDTH].astype(F32).T.astype(BF16)
    channel = lax.broadcasted_iota(jnp.int32, (WIDTH, HEADS * TOKENS), 0) // (WIDTH // HEADS)
    lane = lax.broadcasted_iota(jnp.int32, (WIDTH, HEADS * TOKENS), 1)
    block = (lane >= channel * TOKENS) & (lane < channel * TOKENS + TOKENS)
    scale = (WIDTH // HEADS) ** (-0.5)

    @pl.loop(0, ROWS)
    def _(i):
        mid_n = mid_norm[i]
        rest = jnp.dot(mid_n, att_proj[:, WIDTH:], preferred_element_type=F32)
        key[i] = rest[:, 0:WIDTH].astype(BF16)
        value[i] = rest[:, WIDTH : 2 * WIDTH].astype(BF16)
        att_gate[i] = jax.nn.sigmoid(rest[:, 2 * WIDTH :])
        wide = dot(query_t, jnp.concatenate([mid_n] * HEADS, axis=0), NT)
        query[i] = jnp.where(block, wide * scale, 0.0).astype(BF16)

    ids = lax.broadcasted_iota(jnp.int32, (16, TOKENS), 0)
    one_hot = jnp.where(ids == chain_v[...], 1.0, 0.0).astype(BF16)
    same = dot(one_hot, one_hot, TN)
    absent = 10000.0 * (mask_row - 1.0)

    @pl.loop(0, PARTS)
    def _(step):
        source = other(step)

        @pl.when(step > 0)
        def _():
            arrived(2, recv3, source).wait_recv()

        at = pl.multiple_of(source * 40, 8)
        got = recv3[source].astype(F32)
        bias_m[pl.ds(at, 40), :] = got[0:40]
        for t in range(3):
            size = 16 if t < 2 else 8
            bias_tl[pl.ds(pl.multiple_of(at + 16 * t, 8), size), 0:TAIL] = got[
                48 : 48 + size, TAIL * t : TAIL * t + TAIL
            ]

    mains, rests = [], []
    for h in range(HEADS):
        extra = same_v[0:1, h : h + 1] * same
        every = pl.ds(h, TOKENS, stride=HEADS)
        mains.append(bias_m[every, :] + extra[:, 0:128] + absent[:, 0:128])
        rest = bias_tl[every, :][:, :TAIL] + extra[:, 128:] + absent[:, 128:]
        rests.append(pad_lanes(rest))
    logit[0:128, :] = jnp.concatenate(mains, axis=0).T
    logit[128:TOKENS, :] = jnp.concatenate(rests, axis=0).T[0:TAIL]

    head_of = lax.broadcasted_iota(jnp.int32, (TOKENS, WIDTH), 1) // (WIDTH // HEADS)

    @pl.loop(0, ROWS)
    def _(i):
        scores = jnp.dot(key[i], query[i], preferred_element_type=F32) + logit[...]
        top = jnp.max(scores, axis=0, keepdims=True)
        exps = jnp.exp(scores - top)
        weight = (exps * (1.0 / jnp.sum(exps, axis=0, keepdims=True))).astype(BF16)
        mixes = dot(weight, value[i], TN)
        mixed = mixes[0:TOKENS]
        for h in range(1, HEADS):
            mixed = jnp.where(head_of == h, mixes[h * TOKENS : (h + 1) * TOKENS], mixed)
        gated = (att_gate[i] * mixed).astype(BF16)
        added = jnp.dot(gated, att_out[...], preferred_element_type=F32)
        out[i] = (mid[i].astype(F32) + added).astype(BF16)

    @pl.loop(1, PARTS)
    def _(step):
        part = other(step)
        copy_to(0, send1.at[part], recv1, part).wait_send()
        copy_to(1, send2.at[part], recv2, part).wait_send()
        copy_to(2, send3, recv3, part).wait_send()


def per_device_fused(
    pair, mask, chain, tri_proj, tri_gate, tri_out, att_proj, att_bias, same_chain, att_out
):
    turned = att_bias.T
    high = turned.astype(BF16)
    low = (turned - high.astype(F32)).astype(BF16)
    zeros = jnp.zeros((HEADS, WIDTH), BF16)
    bias_t = jnp.concatenate([high, zeros, low, zeros], axis=0)
    hbm = pl.BlockSpec(memory_space=pltpu.HBM)
    vmem = pl.BlockSpec(memory_space=pltpu.VMEM)
    all_rows = (ROWS, TOKENS, WIDTH)
    inputs = (
        pair,
        tri_proj,
        mask.reshape(1, TOKENS),
        tri_gate,
        tri_out,
        bias_t,
        att_proj,
        chain.reshape(1, TOKENS),
        same_chain.reshape(1, HEADS),
        att_out,
    )
    return pl.pallas_call(
        fused_kernel,
        out_shape=jax.ShapeDtypeStruct(all_rows, BF16),
        in_specs=[hbm] * 10,
        out_specs=vmem,
        scratch_shapes=[pltpu.VMEM(each.shape, each.dtype) for each in inputs]
        + [
            pltpu.VMEM((4 * WIDTH, WIDTH), BF16),
            pltpu.VMEM(all_rows, BF16),
            pltpu.VMEM((ROWS, 2 * WIDTH, TAIL), F32),
            pltpu.VMEM((PARTS, 13, 16, 128), BF16),
            pltpu.VMEM((PARTS, 13, 16, 128), BF16),
            pltpu.VMEM((TOKENS * 16, 128), F32),
            pltpu.VMEM((TOKENS * 16, 128), F32),
            pltpu.VMEM((TOKENS * SHARE, 128), F32),
            pltpu.VMEM((TOKENS * SHARE, 128), F32),
            pltpu.VMEM((PARTS, 112, 128), BF16),
            pltpu.VMEM((PARTS, 112, 128), BF16),
            pltpu.VMEM((PARTS, 112, 128), F32),
            pltpu.VMEM((ROWS, WIDTH, TOKENS), F32),
            pltpu.VMEM(all_rows, F32),
            pltpu.VMEM(all_rows, BF16),
            pltpu.VMEM(all_rows, BF16),
            pltpu.VMEM((40, TOKENS), F32),
            pltpu.VMEM((64, 128), BF16),
            pltpu.VMEM((PARTS, 64, 128), BF16),
            pltpu.VMEM((TOKENS * HEADS, 128), F32),
            pltpu.VMEM((TOKENS * HEADS, 128), F32),
            pltpu.VMEM((TOKENS, HEADS * TOKENS), F32),
            pltpu.VMEM((ROWS, WIDTH, HEADS * TOKENS), BF16),
            pltpu.VMEM(all_rows, BF16),
            pltpu.VMEM(all_rows, BF16),
            pltpu.VMEM(all_rows, F32),
            pltpu.SemaphoreType.DMA((3, PARTS)),
            pltpu.SemaphoreType.DMA((3, PARTS)),
            pltpu.SemaphoreType.DMA((10,)),
        ],
        compiler_params=pltpu.CompilerParams(
            collective_id=0, has_side_effects=True, vmem_limit_bytes=40 * 1024 * 1024
        ),
    )(*inputs)


def per_device(pair, *others):
    fits = pair.shape == (ROWS, TOKENS, WIDTH) and lax.axis_size("row") == PARTS
    return (per_device_fused if fits else per_device_general)(pair, *others)


def solution(mesh):
    return jax.shard_map(
        per_device,
        mesh=mesh,
        in_specs=(
            P(("groups", "row"), None, None),
            P("groups"),
            P("groups"),
            P(),
            P(),
            P(),
            P(),
            P(),
            P(),
            P(),
        ),
        out_specs=P(("groups", "row"), None, None),
        check_vma=False,
    )
```

```python
import jax
import jax.numpy as jnp
from jax import lax
from jax.experimental import pallas as pl
from jax.experimental.pallas import tpu as pltpu
from jax.sharding import PartitionSpec as P

F32 = jnp.float32
BF16 = jnp.bfloat16
NT = (((1,), (1,)), ((), ()))
TN = (((0,), (0,)), ((), ()))


def layer_norm(values):
    centre_mean = jnp.mean(values, axis=-1, keepdims=True)
    centred = values - centre_mean
    spread = jnp.mean(centred * centred, axis=-1, keepdims=True)
    return centred * lax.rsqrt(spread + 1e-05)


def chain_logits(bias_block, same_chain, chain_rows, chain, mask_float):
    same = (chain_rows[:, None] == chain[None, :]).astype(jnp.float32)
    logit_bias = bias_block.astype(jnp.float32) + same_chain[:, None, None] * same[None, :, :]
    return logit_bias + 10000.0 * (mask_float - 1.0)[None, None, :]


def attend(query, att_gate, key, value, logit_bias, head_count, head_size):
    block_len = query.shape[1]
    tokens = key.shape[1]
    width = head_count * head_size

    def one_row(inputs):
        query_row, key_row, value_row, gate_row = inputs
        query_heads = query_row.reshape(block_len, head_count, head_size)
        key_heads = key_row.reshape(tokens, head_count, head_size)
        value_heads = value_row.reshape(tokens, head_count, head_size)
        scores = (
            jnp.einsum("jhd,khd->hjk", query_heads, key_heads, preferred_element_type=jnp.float32)
            + logit_bias
        )
        row_max = jnp.max(scores, axis=2, keepdims=True)
        exp_scores = jnp.exp(scores - row_max)
        weight = (exp_scores / jnp.sum(exp_scores, axis=2, keepdims=True)).astype(jnp.bfloat16)
        mixed_heads = jnp.einsum(
            "hjk,khd->jhd", weight, value_heads, preferred_element_type=jnp.float32
        )
        return (gate_row * mixed_heads.reshape(block_len, width)).astype(jnp.bfloat16)

    return lax.map(one_row, (query, key, value, att_gate))


def per_device_general(
    pair, mask, chain, tri_proj, tri_gate, tri_out, att_proj, att_bias, same_chain, att_out
):
    local_rows, tokens, width = pair.shape
    head_count = same_chain.shape[0]
    head_size = width // head_count
    scale = head_size ** (-0.5)
    part_count = lax.axis_size("row")
    share_width = width // part_count
    first_row = lax.axis_index("row") * local_rows
    mask_float = mask.astype(jnp.float32)
    row_mask = lax.dynamic_slice_in_dim(mask_float, first_row, local_rows)

    def project_row(inputs):
        pair_row, mask_value = inputs
        normed = layer_norm(pair_row.astype(jnp.float32)).astype(jnp.bfloat16)
        projected = jnp.dot(normed, tri_proj, preferred_element_type=jnp.float32)
        weight = (mask_value * mask_float)[:, None]
        left_proj = (
            weight * jax.nn.sigmoid(projected[:, 2 * width : 3 * width]) * projected[:, :width]
        ).astype(jnp.bfloat16)
        right_proj = (
            weight * jax.nn.sigmoid(projected[:, 3 * width :]) * projected[:, width : 2 * width]
        ).astype(jnp.bfloat16)
        out_gate = jax.nn.sigmoid(jnp.dot(normed, tri_gate, preferred_element_type=jnp.float32))
        return (left_proj, right_proj, out_gate)

    left_proj, right_proj, out_gate = lax.map(project_row, (pair, row_mask))
    left_lay = jnp.transpose(left_proj, (2, 0, 1)).reshape(
        part_count, share_width, local_rows, tokens
    )
    right_lay = jnp.transpose(right_proj, (2, 0, 1)).reshape(
        part_count, share_width, local_rows, tokens
    )
    got_left, got_right = (
        lax.all_to_all(left_lay, "row", split_axis=0, concat_axis=2, tiled=True),
        lax.all_to_all(right_lay, "row", split_axis=0, concat_axis=2, tiled=True),
    )
    product = jnp.einsum(
        "cik,cjk->cij", got_left[0], got_right[0], preferred_element_type=jnp.float32
    )
    returned = lax.all_to_all(
        product.astype(jnp.bfloat16)[None], "row", split_axis=2, concat_axis=0, tiled=True
    )
    tri_sum = jnp.transpose(returned.reshape(width, local_rows, tokens), (1, 2, 0))

    def finish_row(inputs):
        pair_row, summed, gate_row = inputs
        tri_norm = layer_norm(summed.astype(jnp.float32)).astype(jnp.bfloat16)
        update = jnp.dot(tri_norm, tri_out, preferred_element_type=jnp.float32)
        mid_pair = (pair_row.astype(jnp.float32) + gate_row * update).astype(jnp.bfloat16)
        mid_norm = layer_norm(mid_pair.astype(jnp.float32)).astype(jnp.bfloat16)
        att_all = jnp.dot(mid_norm, att_proj, preferred_element_type=jnp.float32)
        query = (att_all[:, :width] * scale).astype(jnp.bfloat16)
        key = att_all[:, width : 2 * width].astype(jnp.bfloat16)
        value = att_all[:, 2 * width : 3 * width].astype(jnp.bfloat16)
        att_gate = jax.nn.sigmoid(att_all[:, 3 * width :])
        pair_bias = jnp.dot(mid_norm, att_bias, preferred_element_type=jnp.float32).astype(
            jnp.bfloat16
        )
        return (mid_pair, query, key, value, att_gate, pair_bias)

    mid_pair, query, key, value, att_gate, pair_bias = lax.map(
        finish_row, (pair, tri_sum, out_gate)
    )
    bias_lay = jnp.transpose(pair_bias, (2, 0, 1))
    full_bias = lax.all_gather(bias_lay, "row", axis=1, tiled=True)
    logit_bias = chain_logits(full_bias, same_chain, chain, chain, mask_float)
    gated = attend(query, att_gate, key, value, logit_bias, head_count, head_size)
    projected_out = jnp.dot(gated.reshape(-1, width), att_out, preferred_element_type=jnp.float32)
    return (mid_pair.astype(jnp.float32) + projected_out.reshape(local_rows, tokens, width)).astype(
        jnp.bfloat16
    )


ROWS, TOKENS, WIDTH, PARTS, HEADS = 10, 160, 128, 16, 4
SHARE = WIDTH // PARTS
TAIL = TOKENS - 128


def dot(left, right, dims):
    return lax.dot_general(left, right, dims, preferred_element_type=F32)


def norm(values, axis):
    centred = values - jnp.mean(values, axis=axis, keepdims=True)
    spread = jnp.mean(centred * centred, axis=axis, keepdims=True)
    return (centred * lax.rsqrt(spread + 1e-05)).astype(BF16)


def pad_lanes(values):
    return jnp.concatenate(
        [values, jnp.zeros((values.shape[0], 128 - values.shape[1]), values.dtype)], axis=1
    )


def fused_kernel(
    *refs,
):
    outside, (out, *inside, loads) = refs[:10], refs[10:]
    held, scratch = inside[:10], inside[10:]
    fetches = [
        pltpu.make_async_copy(source, target, loads.at[k])
        for k, (source, target) in enumerate(zip(outside, held))
    ]
    for fetch in fetches:
        fetch.start()
    fused_body(fetches, out, *held, *scratch)


def fused_body(
    fetches,
    out,
    pair,
    tri_proj,
    mask_v,
    tri_gate,
    tri_out,
    bias_v,
    att_proj,
    chain_v,
    same_v,
    att_out,
    proj_t,
    normed,
    tails,
    send1,
    recv1,
    main_f,
    tail_f,
    sum_m,
    sum_t,
    send2,
    recv2,
    recv2_f,
    summed,
    gate,
    mid,
    mid_norm,
    bias_rows,
    send3,
    recv3,
    bias_m,
    bias_tl,
    logit,
    query,
    key,
    value,
    att_gate,
    sends,
    recvs,
):
    me = lax.axis_index("row")

    def other(step):
        return lax.rem(me + step, PARTS)

    barrier = pltpu.get_barrier_semaphore()

    @pl.loop(1, PARTS)
    def _(step):
        pl.semaphore_signal(
            barrier, inc=1, device_id={"row": other(step)}, device_id_type=pl.DeviceIdType.MESH
        )

    def copy_to(phase, source, landing, part):
        return pltpu.make_async_remote_copy(
            src_ref=source,
            dst_ref=landing.at[me],
            send_sem=sends.at[phase, part],
            recv_sem=recvs.at[phase, me],
            device_id={"row": part},
            device_id_type=pl.DeviceIdType.MESH,
        )

    def arrived(phase, landing, source):
        return pltpu.make_async_remote_copy(
            src_ref=landing.at[source],
            dst_ref=landing.at[source],
            send_sem=sends.at[phase, source],
            recv_sem=recvs.at[phase, source],
            device_id={"row": source},
            device_id_type=pl.DeviceIdType.MESH,
        )

    for fetch in fetches[:3]:
        fetch.wait()

    turned = tri_proj[...].astype(F32).T
    pieces = []
    for half in range(2):
        for part in range(PARTS):
            for side in range(2):
                at = half * 2 * WIDTH + side * WIDTH + part * SHARE
                pieces.append(turned[at : at + SHARE])
    proj_t[...] = jnp.concatenate(pieces, axis=0).astype(BF16)
    mask_row = mask_v[...].astype(F32)
    token = lax.broadcasted_iota(jnp.int32, (1, TOKENS), 1)

    @pl.loop(0, ROWS)
    def _(i):
        row = norm(pair[i].astype(F32), 1)
        normed[i] = row
        projected = dot(proj_t[...], row, NT)
        mine = jnp.where(token == me * ROWS + i, mask_row, 0.0)
        weight = mask_row * jnp.sum(mine, axis=1, keepdims=True)
        both = weight * jax.nn.sigmoid(projected[2 * WIDTH :]) * projected[: 2 * WIDTH]
        send1[:, i] = both[:, :128].astype(BF16).reshape(PARTS, 16, 128)
        tails[i] = both[:, 128:]

    for tile in range(3):
        parts = [tails[i] for i in range(4 * tile, min(4 * tile + 4, ROWS))]
        packed = jnp.concatenate(parts, axis=1)
        if len(parts) < 4:
            packed = pad_lanes(packed)
        send1[:, ROWS + tile] = packed.astype(BF16).reshape(PARTS, 16, 128)

    pl.semaphore_wait(barrier, PARTS - 1)

    @pl.loop(1, PARTS)
    def _(step):
        part = other(step)
        copy_to(0, send1.at[part], recv1, part).start()

    recv1[me] = send1[me]
    for fetch in fetches[3:]:
        fetch.wait()

    @pl.loop(0, ROWS)
    def _(i):
        gate[i] = jax.nn.sigmoid(jnp.dot(normed[i], tri_gate[...], preferred_element_type=F32))

    @pl.loop(0, PARTS)
    def _(step):
        source = other(step)

        @pl.when(step > 0)
        def _():
            arrived(0, recv1, source).wait_recv()

        for i in range(ROWS):
            at = pl.multiple_of((source * ROWS + i) * 16, 16)
            main_f[pl.ds(at, 16), :] = recv1[source, i].astype(F32)
            lane = TAIL * (i % 4)
            tail = recv1[source, ROWS + i // 4].astype(F32)[:, lane : lane + TAIL]
            tail_f[pl.ds(at, 16), 0:TAIL] = tail

    for c in range(SHARE):
        at_l, at_r = pl.ds(c, TOKENS, stride=16), pl.ds(SHARE + c, TOKENS, stride=16)
        main = dot(main_f[at_l, :].astype(BF16), main_f[at_r, :].astype(BF16), NT)
        tail = dot(
            tail_f[at_l, :][:, :TAIL].astype(BF16), tail_f[at_r, :][:, :TAIL].astype(BF16), NT
        )
        total = main + tail
        sum_m[pl.ds(c, TOKENS, stride=SHARE), :] = total[:, :128]
        sum_t[pl.ds(c, TOKENS, stride=SHARE), :] = pad_lanes(total[:, 128:])

    @pl.loop(0, PARTS)
    def _(step):
        part = other(step)
        at = pl.multiple_of(part * ROWS * SHARE, ROWS * SHARE)
        send2[part, 0:80] = sum_m[pl.ds(at, 80), :].astype(BF16)
        rest = sum_t[pl.ds(at, 80), :][:, :TAIL]
        packed = jnp.concatenate([rest[16 * t : 16 * t + 16] for t in range(4)], axis=1)
        send2[part, 80:96] = packed.astype(BF16)
        send2[part, 96:112] = pad_lanes(rest[64:80]).astype(BF16)

        @pl.when(step > 0)
        def _():
            copy_to(1, send2.at[part], recv2, part).start()

    recv2[me] = send2[me]

    @pl.loop(0, PARTS)
    def _(step):
        source = other(step)

        @pl.when(step > 0)
        def _():
            arrived(1, recv2, source).wait_recv()

        recv2_f[source] = recv2[source].astype(F32)

    for i in range(ROWS):
        summed[i, :, 0:128] = recv2_f[:, SHARE * i : SHARE * i + SHARE, :].reshape(WIDTH, 128)
        row = 80 + SHARE * (i % 2) + (16 if i >= 8 else 0)
        lane = TAIL * ((i // 2) % 4)
        rest = recv2_f[:, row : row + SHARE, :].reshape(WIDTH, 128)
        summed[i, :, 128:TOKENS] = rest[:, lane : lane + TAIL]

    high = bias_v[...].astype(BF16).astype(F32)
    none = jnp.zeros((HEADS, WIDTH), F32)
    bias_t = jnp.concatenate([high, none, bias_v[...] - high, none], axis=0).astype(BF16)

    @pl.loop(0, ROWS // 2)
    def _(pair_at):
        biases = []
        for half in range(2):
            i = pair_at * 2 + half
            tri_norm = norm(summed[i], 0)
            update = dot(tri_norm, tri_out[...], TN)
            mid_row = (pair[i].astype(F32) + gate[i] * update).astype(BF16)
            mid[i] = mid_row
            mid_n = norm(mid_row.astype(F32), 1)
            mid_norm[i] = mid_n
            bias = dot(bias_t, mid_n, NT)
            biases.append(bias[0:8] + bias[8:16])
        joined = jnp.concatenate([biases[0][0:HEADS], biases[1][0:HEADS]], axis=0)
        bias_rows[pl.ds(pl.multiple_of(pair_at * 8, 8), 8), :] = joined

    send3[0:32] = bias_rows[0:32, 0:128].astype(BF16)
    send3[32:48] = jnp.concatenate(
        [bias_rows[32:40, 0:128], jnp.zeros((8, 128), F32)], axis=0
    ).astype(BF16)
    last = jnp.concatenate([bias_rows[32:40, 128:TOKENS], jnp.zeros((8, TAIL), F32)], axis=0)
    send3[48:64] = pad_lanes(
        jnp.concatenate(
            [bias_rows[0:16, 128:TOKENS], bias_rows[16:32, 128:TOKENS], last], axis=1
        )
    ).astype(BF16)

    @pl.loop(1, PARTS)
    def _(step):
        part = other(step)
        copy_to(2, send3, recv3, part).start()

    recv3[me] = send3[...]

    query_t = att_proj[:, 0:WIDTH].astype(F32).T.astype(BF16)
    channel = lax.broadcasted_iota(jnp.int32, (WIDTH, HEADS * TOKENS), 0) // (WIDTH // HEADS)
    lane = lax.broadcasted_iota(jnp.int32, (WIDTH, HEADS * TOKENS), 1)
    block = (lane >= channel * TOKENS) & (lane < channel * TOKENS + TOKENS)
    scale = (WIDTH // HEADS) ** (-0.5)

    @pl.loop(0, ROWS)
    def _(i):
        mid_n = mid_norm[i]
        rest = jnp.dot(mid_n, att_proj[:, WIDTH:], preferred_element_type=F32)
        key[i] = rest[:, 0:WIDTH].astype(BF16)
        value[i] = rest[:, WIDTH : 2 * WIDTH].astype(BF16)
        att_gate[i] = jax.nn.sigmoid(rest[:, 2 * WIDTH :])
        wide = dot(query_t, jnp.concatenate([mid_n] * HEADS, axis=0), NT)
        query[i] = jnp.where(block, wide * scale, 0.0).astype(BF16)

    ids = lax.broadcasted_iota(jnp.int32, (16, TOKENS), 0)
    one_hot = jnp.where(ids == chain_v[...], 1.0, 0.0).astype(BF16)
    same = dot(one_hot, one_hot, TN)
    absent = 10000.0 * (mask_row - 1.0)

    @pl.loop(0, PARTS)
    def _(step):
        source = other(step)

        @pl.when(step > 0)
        def _():
            arrived(2, recv3, source).wait_recv()

        at = pl.multiple_of(source * 40, 8)
        got = recv3[source].astype(F32)
        bias_m[pl.ds(at, 40), :] = got[0:40]
        for t in range(3):
            size = 16 if t < 2 else 8
            bias_tl[pl.ds(pl.multiple_of(at + 16 * t, 8), size), 0:TAIL] = got[
                48 : 48 + size, TAIL * t : TAIL * t + TAIL
            ]

    mains, rests = [], []
    for h in range(HEADS):
        extra = same_v[0:1, h : h + 1] * same
        every = pl.ds(h, TOKENS, stride=HEADS)
        mains.append(bias_m[every, :] + extra[:, 0:128] + absent[:, 0:128])
        rest = bias_tl[every, :][:, :TAIL] + extra[:, 128:] + absent[:, 128:]
        rests.append(pad_lanes(rest))
    logit[0:128, :] = jnp.concatenate(mains, axis=0).T
    logit[128:TOKENS, :] = jnp.concatenate(rests, axis=0).T[0:TAIL]

    head_of = lax.broadcasted_iota(jnp.int32, (TOKENS, WIDTH), 1) // (WIDTH // HEADS)

    @pl.loop(0, ROWS)
    def _(i):
        scores = jnp.dot(key[i], query[i], preferred_element_type=F32) + logit[...]
        top = jnp.max(scores, axis=0, keepdims=True)
        exps = jnp.exp(scores - top)
        weight = (exps * (1.0 / jnp.sum(exps, axis=0, keepdims=True))).astype(BF16)
        mixes = dot(weight, value[i], TN)
        mixed = mixes[0:TOKENS]
        for h in range(1, HEADS):
            mixed = jnp.where(head_of == h, mixes[h * TOKENS : (h + 1) * TOKENS], mixed)
        gated = (att_gate[i] * mixed).astype(BF16)
        added = jnp.dot(gated, att_out[...], preferred_element_type=F32)
        out[i] = (mid[i].astype(F32) + added).astype(BF16)

    @pl.loop(1, PARTS)
    def _(step):
        part = other(step)
        copy_to(0, send1.at[part], recv1, part).wait_send()
        copy_to(1, send2.at[part], recv2, part).wait_send()
        copy_to(2, send3, recv3, part).wait_send()


def per_device_fused(
    pair, mask, chain, tri_proj, tri_gate, tri_out, att_proj, att_bias, same_chain, att_out
):
    hbm = pl.BlockSpec(memory_space=pltpu.HBM)
    vmem = pl.BlockSpec(memory_space=pltpu.VMEM)
    all_rows = (ROWS, TOKENS, WIDTH)
    inputs = (
        pair,
        tri_proj,
        mask.reshape(1, TOKENS),
        tri_gate,
        tri_out,
        att_bias.T,
        att_proj,
        chain.reshape(1, TOKENS),
        same_chain.reshape(1, HEADS),
        att_out,
    )
    return pl.pallas_call(
        fused_kernel,
        out_shape=jax.ShapeDtypeStruct(all_rows, BF16),
        in_specs=[hbm] * 10,
        out_specs=vmem,
        scratch_shapes=[pltpu.VMEM(each.shape, each.dtype) for each in inputs]
        + [
            pltpu.VMEM((4 * WIDTH, WIDTH), BF16),
            pltpu.VMEM(all_rows, BF16),
            pltpu.VMEM((ROWS, 2 * WIDTH, TAIL), F32),
            pltpu.VMEM((PARTS, 13, 16, 128), BF16),
            pltpu.VMEM((PARTS, 13, 16, 128), BF16),
            pltpu.VMEM((TOKENS * 16, 128), F32),
            pltpu.VMEM((TOKENS * 16, 128), F32),
            pltpu.VMEM((TOKENS * SHARE, 128), F32),
            pltpu.VMEM((TOKENS * SHARE, 128), F32),
            pltpu.VMEM((PARTS, 112, 128), BF16),
            pltpu.VMEM((PARTS, 112, 128), BF16),
            pltpu.VMEM((PARTS, 112, 128), F32),
            pltpu.VMEM((ROWS, WIDTH, TOKENS), F32),
            pltpu.VMEM(all_rows, F32),
            pltpu.VMEM(all_rows, BF16),
            pltpu.VMEM(all_rows, BF16),
            pltpu.VMEM((40, TOKENS), F32),
            pltpu.VMEM((64, 128), BF16),
            pltpu.VMEM((PARTS, 64, 128), BF16),
            pltpu.VMEM((TOKENS * HEADS, 128), F32),
            pltpu.VMEM((TOKENS * HEADS, 128), F32),
            pltpu.VMEM((TOKENS, HEADS * TOKENS), F32),
            pltpu.VMEM((ROWS, WIDTH, HEADS * TOKENS), BF16),
            pltpu.VMEM(all_rows, BF16),
            pltpu.VMEM(all_rows, BF16),
            pltpu.VMEM(all_rows, F32),
            pltpu.SemaphoreType.DMA((3, PARTS)),
            pltpu.SemaphoreType.DMA((3, PARTS)),
            pltpu.SemaphoreType.DMA((10,)),
        ],
        compiler_params=pltpu.CompilerParams(
            collective_id=0, has_side_effects=True, vmem_limit_bytes=64 * 1024 * 1024
        ),
    )(*inputs)


def per_device(pair, *others):
    fits = pair.shape == (ROWS, TOKENS, WIDTH) and lax.axis_size("row") == PARTS
    return (per_device_fused if fits else per_device_general)(pair, *others)


def solution(mesh):
    return jax.shard_map(
        per_device,
        mesh=mesh,
        in_specs=(
            P(("groups", "row"), None, None),
            P("groups"),
            P("groups"),
            P(),
            P(),
            P(),
            P(),
            P(),
            P(),
            P(),
        ),
        out_specs=P(("groups", "row"), None, None),
        check_vma=False,
    )
```

```python
import jax
import jax.numpy as jnp
from jax import lax
from jax.experimental import pallas as pl
from jax.experimental.pallas import tpu as pltpu
from jax.sharding import PartitionSpec as P

F32 = jnp.float32
BF16 = jnp.bfloat16
NT = (((1,), (1,)), ((), ()))
TN = (((0,), (0,)), ((), ()))


def layer_norm(values):
    centre_mean = jnp.mean(values, axis=-1, keepdims=True)
    centred = values - centre_mean
    spread = jnp.mean(centred * centred, axis=-1, keepdims=True)
    return centred * lax.rsqrt(spread + 1e-05)


def chain_logits(bias_block, same_chain, chain_rows, chain, mask_float):
    same = (chain_rows[:, None] == chain[None, :]).astype(jnp.float32)
    logit_bias = bias_block.astype(jnp.float32) + same_chain[:, None, None] * same[None, :, :]
    return logit_bias + 10000.0 * (mask_float - 1.0)[None, None, :]


def attend(query, att_gate, key, value, logit_bias, head_count, head_size):
    block_len = query.shape[1]
    tokens = key.shape[1]
    width = head_count * head_size

    def one_row(inputs):
        query_row, key_row, value_row, gate_row = inputs
        query_heads = query_row.reshape(block_len, head_count, head_size)
        key_heads = key_row.reshape(tokens, head_count, head_size)
        value_heads = value_row.reshape(tokens, head_count, head_size)
        scores = (
            jnp.einsum("jhd,khd->hjk", query_heads, key_heads, preferred_element_type=jnp.float32)
            + logit_bias
        )
        row_max = jnp.max(scores, axis=2, keepdims=True)
        exp_scores = jnp.exp(scores - row_max)
        weight = (exp_scores / jnp.sum(exp_scores, axis=2, keepdims=True)).astype(jnp.bfloat16)
        mixed_heads = jnp.einsum(
            "hjk,khd->jhd", weight, value_heads, preferred_element_type=jnp.float32
        )
        return (gate_row * mixed_heads.reshape(block_len, width)).astype(jnp.bfloat16)

    return lax.map(one_row, (query, key, value, att_gate))


def per_device_general(
    pair, mask, chain, tri_proj, tri_gate, tri_out, att_proj, att_bias, same_chain, att_out
):
    local_rows, tokens, width = pair.shape
    head_count = same_chain.shape[0]
    head_size = width // head_count
    scale = head_size ** (-0.5)
    part_count = lax.axis_size("row")
    share_width = width // part_count
    first_row = lax.axis_index("row") * local_rows
    mask_float = mask.astype(jnp.float32)
    row_mask = lax.dynamic_slice_in_dim(mask_float, first_row, local_rows)

    def project_row(inputs):
        pair_row, mask_value = inputs
        normed = layer_norm(pair_row.astype(jnp.float32)).astype(jnp.bfloat16)
        projected = jnp.dot(normed, tri_proj, preferred_element_type=jnp.float32)
        weight = (mask_value * mask_float)[:, None]
        left_proj = (
            weight * jax.nn.sigmoid(projected[:, 2 * width : 3 * width]) * projected[:, :width]
        ).astype(jnp.bfloat16)
        right_proj = (
            weight * jax.nn.sigmoid(projected[:, 3 * width :]) * projected[:, width : 2 * width]
        ).astype(jnp.bfloat16)
        out_gate = jax.nn.sigmoid(jnp.dot(normed, tri_gate, preferred_element_type=jnp.float32))
        return (left_proj, right_proj, out_gate)

    left_proj, right_proj, out_gate = lax.map(project_row, (pair, row_mask))
    left_lay = jnp.transpose(left_proj, (2, 0, 1)).reshape(
        part_count, share_width, local_rows, tokens
    )
    right_lay = jnp.transpose(right_proj, (2, 0, 1)).reshape(
        part_count, share_width, local_rows, tokens
    )
    got_left, got_right = (
        lax.all_to_all(left_lay, "row", split_axis=0, concat_axis=2, tiled=True),
        lax.all_to_all(right_lay, "row", split_axis=0, concat_axis=2, tiled=True),
    )
    product = jnp.einsum(
        "cik,cjk->cij", got_left[0], got_right[0], preferred_element_type=jnp.float32
    )
    returned = lax.all_to_all(
        product.astype(jnp.bfloat16)[None], "row", split_axis=2, concat_axis=0, tiled=True
    )
    tri_sum = jnp.transpose(returned.reshape(width, local_rows, tokens), (1, 2, 0))

    def finish_row(inputs):
        pair_row, summed, gate_row = inputs
        tri_norm = layer_norm(summed.astype(jnp.float32)).astype(jnp.bfloat16)
        update = jnp.dot(tri_norm, tri_out, preferred_element_type=jnp.float32)
        mid_pair = (pair_row.astype(jnp.float32) + gate_row * update).astype(jnp.bfloat16)
        mid_norm = layer_norm(mid_pair.astype(jnp.float32)).astype(jnp.bfloat16)
        att_all = jnp.dot(mid_norm, att_proj, preferred_element_type=jnp.float32)
        query = (att_all[:, :width] * scale).astype(jnp.bfloat16)
        key = att_all[:, width : 2 * width].astype(jnp.bfloat16)
        value = att_all[:, 2 * width : 3 * width].astype(jnp.bfloat16)
        att_gate = jax.nn.sigmoid(att_all[:, 3 * width :])
        pair_bias = jnp.dot(mid_norm, att_bias, preferred_element_type=jnp.float32).astype(
            jnp.bfloat16
        )
        return (mid_pair, query, key, value, att_gate, pair_bias)

    mid_pair, query, key, value, att_gate, pair_bias = lax.map(
        finish_row, (pair, tri_sum, out_gate)
    )
    bias_lay = jnp.transpose(pair_bias, (2, 0, 1))
    full_bias = lax.all_gather(bias_lay, "row", axis=1, tiled=True)
    logit_bias = chain_logits(full_bias, same_chain, chain, chain, mask_float)
    gated = attend(query, att_gate, key, value, logit_bias, head_count, head_size)
    projected_out = jnp.dot(gated.reshape(-1, width), att_out, preferred_element_type=jnp.float32)
    return (mid_pair.astype(jnp.float32) + projected_out.reshape(local_rows, tokens, width)).astype(
        jnp.bfloat16
    )


ROWS, TOKENS, WIDTH, PARTS, HEADS = 10, 160, 128, 16, 4
NEAR = PARTS // 2
SHARE = WIDTH // NEAR
TILES = 13
EARLY = 5
TAIL = TOKENS - 128


def dot(left, right, dims):
    return lax.dot_general(left, right, dims, preferred_element_type=F32)


def norm(values, axis):
    centred = values - jnp.mean(values, axis=axis, keepdims=True)
    spread = jnp.mean(centred * centred, axis=axis, keepdims=True)
    return (centred * lax.rsqrt(spread + 1e-05)).astype(BF16)


def pad_lanes(values):
    return jnp.concatenate(
        [values, jnp.zeros((values.shape[0], 128 - values.shape[1]), values.dtype)], axis=1
    )


def fused_kernel(
    *refs,
):
    outside, (out, *inside, loads) = refs[:10], refs[10:]
    held, scratch = inside[:10], inside[10:]
    fetches = [
        pltpu.make_async_copy(source, target, loads.at[k])
        for k, (source, target) in enumerate(zip(outside, held))
    ]
    for fetch in fetches:
        fetch.start()
    fused_body(fetches, out, *held, *scratch)


def fused_body(
    fetches,
    out,
    pair,
    tri_proj,
    mask_v,
    tri_gate,
    tri_out,
    bias_v,
    att_proj,
    chain_v,
    same_v,
    att_out,
    proj_t,
    normed,
    tails,
    send_l,
    recv_l,
    send_r,
    recv_r,
    left_m,
    left_t,
    right_m,
    right_t,
    sum_m,
    sum_t,
    send2,
    recv2,
    summed,
    gate,
    mid,
    mid_norm,
    bias_rows,
    send3,
    recv3,
    bias_m,
    bias_tl,
    logit,
    query,
    key,
    value,
    att_gate,
    sends,
    recvs,
):
    me = lax.axis_index("row")

    place = lax.rem(me, NEAR)
    first = me - place

    def other(step):
        return lax.rem(me + step, PARTS)

    def near(step):
        return lax.rem(place + step, NEAR)

    barrier = pltpu.get_barrier_semaphore()

    @pl.loop(1, PARTS)
    def _(step):
        pl.semaphore_signal(
            barrier, inc=1, device_id={"row": other(step)}, device_id_type=pl.DeviceIdType.MESH
        )

    def copy_to(sent, phase, source, landing, slot, part):
        return pltpu.make_async_remote_copy(
            src_ref=source,
            dst_ref=landing.at[slot],
            send_sem=sends.at[sent, part],
            recv_sem=recvs.at[phase, slot],
            device_id={"row": part},
            device_id_type=pl.DeviceIdType.MESH,
        )

    def arrived(phase, landing, slot):
        return pltpu.make_async_remote_copy(
            src_ref=landing.at[slot],
            dst_ref=landing.at[slot],
            send_sem=sends.at[phase, slot],
            recv_sem=recvs.at[phase, slot],
            device_id={"row": other(1)},
            device_id_type=pl.DeviceIdType.MESH,
        )

    def right_copy(part):
        return copy_to(0, 0, send_r.at[lax.rem(part, NEAR)], recv_r, me, part)

    def sum_copy(slot):
        return copy_to(1, 1, send2.at[slot], recv2, place, first + slot)

    def bias_copy(part):
        return copy_to(2, 2, send3, recv3, me, part)

    def left_copy(slot):
        return copy_to(3, 3, send_l.at[slot], recv_l, place, first + slot)

    def passed_copy(slot):
        return copy_to(4, 2, recv3.at[across], recv3, across, first + slot)

    across = lax.rem(me + NEAR, PARTS)

    for fetch in fetches[:3]:
        fetch.wait()

    proj_t[...] = tri_proj[...].astype(F32).T.astype(BF16)
    mask_row = mask_v[...].astype(F32)
    token = lax.broadcasted_iota(jnp.int32, (1, TOKENS), 1)

    @pl.loop(0, ROWS)
    def _(i):
        row = norm(pair[i].astype(F32), 1)
        normed[i] = row
        projected = dot(proj_t[...], row, NT)
        mine = jnp.where(token == me * ROWS + i, mask_row, 0.0)
        weight = mask_row * jnp.sum(mine, axis=1, keepdims=True)
        both = weight * jax.nn.sigmoid(projected[2 * WIDTH :]) * projected[: 2 * WIDTH]
        main = both[:, :128].astype(BF16)
        send_l[:, i] = main[:WIDTH].reshape(NEAR, SHARE, 128)
        send_r[:, i] = main[WIDTH:].reshape(NEAR, SHARE, 128)
        tails[i] = both[:, 128:]

    for tile in range(3):
        parts = [tails[i] for i in range(4 * tile, min(4 * tile + 4, ROWS))]
        packed = jnp.concatenate(parts, axis=1)
        if len(parts) < 4:
            packed = pad_lanes(packed)
        packed = packed.astype(BF16)
        send_l[:, ROWS + tile] = packed[:WIDTH].reshape(NEAR, SHARE, 128)
        send_r[:, ROWS + tile] = packed[WIDTH:].reshape(NEAR, SHARE, 128)

    pl.semaphore_wait(barrier, PARTS - 1)

    @pl.loop(0, NEAR)
    def _(step):
        right_copy(lax.rem(across - place + near(step), PARTS)).start()

    @pl.loop(1, NEAR)
    def _(step):
        right_copy(first + near(step)).start()
        left_copy(near(step)).start()

    recv_l[place] = send_l[place]
    recv_r[me] = send_r[place]
    for fetch in fetches[3:]:
        fetch.wait()

    @pl.loop(0, ROWS)
    def _(i):
        gate[i] = jax.nn.sigmoid(jnp.dot(normed[i], tri_gate[...], preferred_element_type=F32))

    def unpack(landing, slot, main_f, tail_f):
        for i in range(ROWS):
            at = pl.ds(pl.multiple_of((slot * ROWS + i) * SHARE, SHARE), SHARE)
            main_f[at, :] = landing[slot, i].astype(F32)
            lane = TAIL * (i % 4)
            tail = landing[slot, ROWS + i // 4].astype(F32)[:, lane : lane + TAIL]
            tail_f[at, 0:TAIL] = tail

    @pl.loop(0, NEAR)
    def _(step):
        slot = near(step)

        @pl.when(step > 0)
        def _():
            arrived(3, recv_l, slot).wait_recv()
            arrived(0, recv_r, first + slot).wait_recv()

        unpack(recv_l, slot, left_m, left_t)
        unpack(recv_r, first + slot, right_m, right_t)

    @pl.loop(0, NEAR)
    def _(step):
        source = across - place + near(step)
        arrived(0, recv_r, source).wait_recv()
        unpack(recv_r, source, right_m, right_t)

    for c in range(SHARE):
        at_l, at_r = pl.ds(c, TOKENS // 2, stride=SHARE), pl.ds(c, TOKENS, stride=SHARE)
        main = dot(left_m[at_l, :].astype(BF16), right_m[at_r, :].astype(BF16), NT)
        tail = dot(
            left_t[at_l, :][:, :TAIL].astype(BF16), right_t[at_r, :][:, :TAIL].astype(BF16), NT
        )
        total = main + tail
        sum_m[at_l, :] = total[:, :128]
        sum_t[at_l, :] = pad_lanes(total[:, 128:])

    @pl.loop(0, NEAR)
    def _(step):
        slot = near(step)
        at = pl.ds(pl.multiple_of(slot * ROWS * SHARE, ROWS * SHARE), ROWS * SHARE)
        send2[slot, 0:ROWS] = sum_m[at, :].astype(BF16).reshape(ROWS, SHARE, 128)
        rest = sum_t[at, :][:, :TAIL]
        for tile in range(3):
            parts = [rest[SHARE * i : SHARE * i + SHARE] for i in range(4 * tile, min(4 * tile + 4, ROWS))]
            packed = jnp.concatenate(parts, axis=1)
            if len(parts) < 4:
                packed = pad_lanes(packed)
            send2[slot, ROWS + tile] = packed.astype(BF16)

        @pl.when(step > 0)
        def _():
            sum_copy(slot).start()

    recv2[place] = send2[place]

    @pl.loop(1, NEAR)
    def _(step):
        arrived(1, recv2, near(step)).wait_recv()

    for i in range(ROWS):
        summed[i, :, 0:128] = recv2[:, i].astype(F32).reshape(WIDTH, 128)
        lane = TAIL * (i % 4)
        rest = recv2[:, ROWS + i // 4].astype(F32).reshape(WIDTH, 128)
        summed[i, :, 128:TOKENS] = rest[:, lane : lane + TAIL]

    high = bias_v[...].astype(BF16).astype(F32)
    none = jnp.zeros((HEADS, WIDTH), F32)
    bias_t = jnp.concatenate([high, none, bias_v[...] - high, none], axis=0).astype(BF16)

    @pl.loop(0, ROWS // 2)
    def _(pair_at):
        biases = []
        for half in range(2):
            i = pair_at * 2 + half
            tri_norm = norm(summed[i], 0)
            update = dot(tri_norm, tri_out[...], TN)
            mid_row = (pair[i].astype(F32) + gate[i] * update).astype(BF16)
            mid[i] = mid_row
            mid_n = norm(mid_row.astype(F32), 1)
            mid_norm[i] = mid_n
            bias = dot(bias_t, mid_n, NT)
            biases.append(bias[0:8] + bias[8:16])
        joined = jnp.concatenate([biases[0][0:HEADS], biases[1][0:HEADS]], axis=0)
        bias_rows[pl.ds(pl.multiple_of(pair_at * 8, 8), 8), :] = joined

    send3[0:32] = bias_rows[0:32, 0:128].astype(BF16)
    send3[32:48] = jnp.concatenate(
        [bias_rows[32:40, 0:128], jnp.zeros((8, 128), F32)], axis=0
    ).astype(BF16)
    last = jnp.concatenate([bias_rows[32:40, 128:TOKENS], jnp.zeros((8, TAIL), F32)], axis=0)
    send3[48:64] = pad_lanes(
        jnp.concatenate(
            [bias_rows[0:16, 128:TOKENS], bias_rows[16:32, 128:TOKENS], last], axis=1
        )
    ).astype(BF16)

    bias_copy(across).start()

    @pl.loop(1, NEAR)
    def _(step):
        bias_copy(first + near(step)).start()

    recv3[me] = send3[...]

    query_t = att_proj[:, 0:WIDTH].astype(F32).T.astype(BF16)
    channel = lax.broadcasted_iota(jnp.int32, (WIDTH, HEADS * TOKENS), 0) // (WIDTH // HEADS)
    lane = lax.broadcasted_iota(jnp.int32, (WIDTH, HEADS * TOKENS), 1)
    block = (lane >= channel * TOKENS) & (lane < channel * TOKENS + TOKENS)
    scale = (WIDTH // HEADS) ** (-0.5)

    def attention_inputs(i):
        mid_n = mid_norm[i]
        rest = jnp.dot(mid_n, att_proj[:, WIDTH:], preferred_element_type=F32)
        key[i] = rest[:, 0:WIDTH].astype(BF16)
        value[i] = rest[:, WIDTH : 2 * WIDTH].astype(BF16)
        att_gate[i] = jax.nn.sigmoid(rest[:, 2 * WIDTH :])
        wide = dot(query_t, jnp.concatenate([mid_n] * HEADS, axis=0), NT)
        query[i] = jnp.where(block, wide * scale, 0.0).astype(BF16)

    pl.loop(0, EARLY)(attention_inputs)
    arrived(2, recv3, across).wait_recv()

    @pl.loop(1, NEAR)
    def _(step):
        passed_copy(near(step)).start()

    pl.loop(EARLY, ROWS)(attention_inputs)

    ids = lax.broadcasted_iota(jnp.int32, (16, TOKENS), 0)
    one_hot = jnp.where(ids == chain_v[...], 1.0, 0.0).astype(BF16)
    same = dot(one_hot, one_hot, TN)
    absent = 10000.0 * (mask_row - 1.0)

    @pl.loop(0, PARTS)
    def _(step):
        source = other(step)

        @pl.when((step > 0) & (step != NEAR))
        def _():
            arrived(2, recv3, source).wait_recv()

        at = pl.multiple_of(source * 40, 8)
        got = recv3[source].astype(F32)
        bias_m[pl.ds(at, 40), :] = got[0:40]
        for t in range(3):
            size = 16 if t < 2 else 8
            bias_tl[pl.ds(pl.multiple_of(at + 16 * t, 8), size), 0:TAIL] = got[
                48 : 48 + size, TAIL * t : TAIL * t + TAIL
            ]

    mains, rests = [], []
    for h in range(HEADS):
        extra = same_v[0:1, h : h + 1] * same
        every = pl.ds(h, TOKENS, stride=HEADS)
        mains.append(bias_m[every, :] + extra[:, 0:128] + absent[:, 0:128])
        rest = bias_tl[every, :][:, :TAIL] + extra[:, 128:] + absent[:, 128:]
        rests.append(pad_lanes(rest))
    logit[0:128, :] = jnp.concatenate(mains, axis=0).T
    logit[128:TOKENS, :] = jnp.concatenate(rests, axis=0).T[0:TAIL]

    head_of = lax.broadcasted_iota(jnp.int32, (TOKENS, WIDTH), 1) // (WIDTH // HEADS)

    @pl.loop(0, ROWS)
    def _(i):
        scores = jnp.dot(key[i], query[i], preferred_element_type=F32) + logit[...]
        top = jnp.max(scores, axis=0, keepdims=True)
        exps = jnp.exp(scores - top)
        weight = (exps * (1.0 / jnp.sum(exps, axis=0, keepdims=True))).astype(BF16)
        mixes = dot(weight, value[i], TN)
        mixed = mixes[0:TOKENS]
        for h in range(1, HEADS):
            mixed = jnp.where(head_of == h, mixes[h * TOKENS : (h + 1) * TOKENS], mixed)
        gated = (att_gate[i] * mixed).astype(BF16)
        added = jnp.dot(gated, att_out[...], preferred_element_type=F32)
        out[i] = (mid[i].astype(F32) + added).astype(BF16)

    @pl.loop(1, PARTS)
    def _(step):
        right_copy(other(step)).wait_send()

    bias_copy(across).wait_send()

    @pl.loop(1, NEAR)
    def _(step):
        slot = near(step)
        left_copy(slot).wait_send()
        sum_copy(slot).wait_send()
        bias_copy(first + slot).wait_send()
        passed_copy(slot).wait_send()


def per_device_fused(
    pair, mask, chain, tri_proj, tri_gate, tri_out, att_proj, att_bias, same_chain, att_out
):
    hbm = pl.BlockSpec(memory_space=pltpu.HBM)
    vmem = pl.BlockSpec(memory_space=pltpu.VMEM)
    all_rows = (ROWS, TOKENS, WIDTH)
    inputs = (
        pair,
        tri_proj,
        mask.reshape(1, TOKENS),
        tri_gate,
        tri_out,
        att_bias.T,
        att_proj,
        chain.reshape(1, TOKENS),
        same_chain.reshape(1, HEADS),
        att_out,
    )
    return pl.pallas_call(
        fused_kernel,
        out_shape=jax.ShapeDtypeStruct(all_rows, BF16),
        in_specs=[hbm] * 10,
        out_specs=vmem,
        scratch_shapes=[pltpu.VMEM(each.shape, each.dtype) for each in inputs]
        + [
            pltpu.VMEM((4 * WIDTH, WIDTH), BF16),
            pltpu.VMEM(all_rows, BF16),
            pltpu.VMEM((ROWS, 2 * WIDTH, TAIL), F32),
            pltpu.VMEM((NEAR, TILES, SHARE, 128), BF16),
            pltpu.VMEM((NEAR, TILES, SHARE, 128), BF16),
            pltpu.VMEM((NEAR, TILES, SHARE, 128), BF16),
            pltpu.VMEM((PARTS, TILES, SHARE, 128), BF16),
            pltpu.VMEM((TOKENS // 2 * SHARE, 128), F32),
            pltpu.VMEM((TOKENS // 2 * SHARE, 128), F32),
            pltpu.VMEM((TOKENS * SHARE, 128), F32),
            pltpu.VMEM((TOKENS * SHARE, 128), F32),
            pltpu.VMEM((TOKENS // 2 * SHARE, 128), F32),
            pltpu.VMEM((TOKENS // 2 * SHARE, 128), F32),
            pltpu.VMEM((NEAR, TILES, SHARE, 128), BF16),
            pltpu.VMEM((NEAR, TILES, SHARE, 128), BF16),
            pltpu.VMEM((ROWS, WIDTH, TOKENS), F32),
            pltpu.VMEM(all_rows, F32),
            pltpu.VMEM(all_rows, BF16),
            pltpu.VMEM(all_rows, BF16),
            pltpu.VMEM((40, TOKENS), F32),
            pltpu.VMEM((64, 128), BF16),
            pltpu.VMEM((PARTS, 64, 128), BF16),
            pltpu.VMEM((TOKENS * HEADS, 128), F32),
            pltpu.VMEM((TOKENS * HEADS, 128), F32),
            pltpu.VMEM((TOKENS, HEADS * TOKENS), F32),
            pltpu.VMEM((ROWS, WIDTH, HEADS * TOKENS), BF16),
            pltpu.VMEM(all_rows, BF16),
            pltpu.VMEM(all_rows, BF16),
            pltpu.VMEM(all_rows, F32),
            pltpu.SemaphoreType.DMA((5, PARTS)),
            pltpu.SemaphoreType.DMA((5, PARTS)),
            pltpu.SemaphoreType.DMA((10,)),
        ],
        compiler_params=pltpu.CompilerParams(
            collective_id=0, has_side_effects=True, vmem_limit_bytes=64 * 1024 * 1024
        ),
    )(*inputs)


def per_device(pair, *others):
    fits = pair.shape == (ROWS, TOKENS, WIDTH) and lax.axis_size("row") == PARTS
    return (per_device_fused if fits else per_device_general)(pair, *others)


def solution(mesh):
    return jax.shard_map(
        per_device,
        mesh=mesh,
        in_specs=(
            P(("groups", "row"), None, None),
            P("groups"),
            P("groups"),
            P(),
            P(),
            P(),
            P(),
            P(),
            P(),
            P(),
        ),
        out_specs=P(("groups", "row"), None, None),
        check_vma=False,
    )
```

```python
import jax
import jax.numpy as jnp
from jax import lax
from jax.experimental import pallas as pl
from jax.experimental.pallas import tpu as pltpu
from jax.sharding import PartitionSpec as P

F32 = jnp.float32
BF16 = jnp.bfloat16
NT = (((1,), (1,)), ((), ()))
TN = (((0,), (0,)), ((), ()))


def layer_norm(values):
    centre_mean = jnp.mean(values, axis=-1, keepdims=True)
    centred = values - centre_mean
    spread = jnp.mean(centred * centred, axis=-1, keepdims=True)
    return centred * lax.rsqrt(spread + 1e-05)


def chain_logits(bias_block, same_chain, chain_rows, chain, mask_float):
    same = (chain_rows[:, None] == chain[None, :]).astype(jnp.float32)
    logit_bias = bias_block.astype(jnp.float32) + same_chain[:, None, None] * same[None, :, :]
    return logit_bias + 10000.0 * (mask_float - 1.0)[None, None, :]


def attend(query, att_gate, key, value, logit_bias, head_count, head_size):
    block_len = query.shape[1]
    tokens = key.shape[1]
    width = head_count * head_size

    def one_row(inputs):
        query_row, key_row, value_row, gate_row = inputs
        query_heads = query_row.reshape(block_len, head_count, head_size)
        key_heads = key_row.reshape(tokens, head_count, head_size)
        value_heads = value_row.reshape(tokens, head_count, head_size)
        scores = (
            jnp.einsum("jhd,khd->hjk", query_heads, key_heads, preferred_element_type=jnp.float32)
            + logit_bias
        )
        row_max = jnp.max(scores, axis=2, keepdims=True)
        exp_scores = jnp.exp(scores - row_max)
        weight = (exp_scores / jnp.sum(exp_scores, axis=2, keepdims=True)).astype(jnp.bfloat16)
        mixed_heads = jnp.einsum(
            "hjk,khd->jhd", weight, value_heads, preferred_element_type=jnp.float32
        )
        return (gate_row * mixed_heads.reshape(block_len, width)).astype(jnp.bfloat16)

    return lax.map(one_row, (query, key, value, att_gate))


def per_device_general(
    pair, mask, chain, tri_proj, tri_gate, tri_out, att_proj, att_bias, same_chain, att_out
):
    local_rows, tokens, width = pair.shape
    head_count = same_chain.shape[0]
    head_size = width // head_count
    scale = head_size ** (-0.5)
    part_count = lax.axis_size("row")
    share_width = width // part_count
    first_row = lax.axis_index("row") * local_rows
    mask_float = mask.astype(jnp.float32)
    row_mask = lax.dynamic_slice_in_dim(mask_float, first_row, local_rows)

    def project_row(inputs):
        pair_row, mask_value = inputs
        normed = layer_norm(pair_row.astype(jnp.float32)).astype(jnp.bfloat16)
        projected = jnp.dot(normed, tri_proj, preferred_element_type=jnp.float32)
        weight = (mask_value * mask_float)[:, None]
        left_proj = (
            weight * jax.nn.sigmoid(projected[:, 2 * width : 3 * width]) * projected[:, :width]
        ).astype(jnp.bfloat16)
        right_proj = (
            weight * jax.nn.sigmoid(projected[:, 3 * width :]) * projected[:, width : 2 * width]
        ).astype(jnp.bfloat16)
        out_gate = jax.nn.sigmoid(jnp.dot(normed, tri_gate, preferred_element_type=jnp.float32))
        return (left_proj, right_proj, out_gate)

    left_proj, right_proj, out_gate = lax.map(project_row, (pair, row_mask))
    left_lay = jnp.transpose(left_proj, (2, 0, 1)).reshape(
        part_count, share_width, local_rows, tokens
    )
    right_lay = jnp.transpose(right_proj, (2, 0, 1)).reshape(
        part_count, share_width, local_rows, tokens
    )
    got_left, got_right = (
        lax.all_to_all(left_lay, "row", split_axis=0, concat_axis=2, tiled=True),
        lax.all_to_all(right_lay, "row", split_axis=0, concat_axis=2, tiled=True),
    )
    product = jnp.einsum(
        "cik,cjk->cij", got_left[0], got_right[0], preferred_element_type=jnp.float32
    )
    returned = lax.all_to_all(
        product.astype(jnp.bfloat16)[None], "row", split_axis=2, concat_axis=0, tiled=True
    )
    tri_sum = jnp.transpose(returned.reshape(width, local_rows, tokens), (1, 2, 0))

    def finish_row(inputs):
        pair_row, summed, gate_row = inputs
        tri_norm = layer_norm(summed.astype(jnp.float32)).astype(jnp.bfloat16)
        update = jnp.dot(tri_norm, tri_out, preferred_element_type=jnp.float32)
        mid_pair = (pair_row.astype(jnp.float32) + gate_row * update).astype(jnp.bfloat16)
        mid_norm = layer_norm(mid_pair.astype(jnp.float32)).astype(jnp.bfloat16)
        att_all = jnp.dot(mid_norm, att_proj, preferred_element_type=jnp.float32)
        query = (att_all[:, :width] * scale).astype(jnp.bfloat16)
        key = att_all[:, width : 2 * width].astype(jnp.bfloat16)
        value = att_all[:, 2 * width : 3 * width].astype(jnp.bfloat16)
        att_gate = jax.nn.sigmoid(att_all[:, 3 * width :])
        pair_bias = jnp.dot(mid_norm, att_bias, preferred_element_type=jnp.float32).astype(
            jnp.bfloat16
        )
        return (mid_pair, query, key, value, att_gate, pair_bias)

    mid_pair, query, key, value, att_gate, pair_bias = lax.map(
        finish_row, (pair, tri_sum, out_gate)
    )
    bias_lay = jnp.transpose(pair_bias, (2, 0, 1))
    full_bias = lax.all_gather(bias_lay, "row", axis=1, tiled=True)
    logit_bias = chain_logits(full_bias, same_chain, chain, chain, mask_float)
    gated = attend(query, att_gate, key, value, logit_bias, head_count, head_size)
    projected_out = jnp.dot(gated.reshape(-1, width), att_out, preferred_element_type=jnp.float32)
    return (mid_pair.astype(jnp.float32) + projected_out.reshape(local_rows, tokens, width)).astype(
        jnp.bfloat16
    )


ROWS, TOKENS, WIDTH, PARTS, HEADS = 10, 160, 128, 16, 4
NEAR = PARTS // 2
SHARE = WIDTH // NEAR
TILES = 13
EARLY = 5
TAIL = TOKENS - 128


def dot(left, right, dims):
    return lax.dot_general(left, right, dims, preferred_element_type=F32)


def norm(values, axis):
    centred = values - jnp.mean(values, axis=axis, keepdims=True)
    spread = jnp.mean(centred * centred, axis=axis, keepdims=True)
    return (centred * lax.rsqrt(spread + 1e-05)).astype(BF16)


def pad_lanes(values):
    return jnp.concatenate(
        [values, jnp.zeros((values.shape[0], 128 - values.shape[1]), values.dtype)], axis=1
    )


def fused_kernel(
    *refs,
):
    outside, (out, *inside, loads) = refs[:10], refs[10:]
    held, scratch = inside[:10], inside[10:]
    fetches = [
        pltpu.make_async_copy(source, target, loads.at[k])
        for k, (source, target) in enumerate(zip(outside, held))
    ]
    for fetch in fetches:
        fetch.start()
    fused_body(fetches, out, *held, *scratch)


def fused_body(
    fetches,
    out,
    pair,
    tri_proj,
    mask_v,
    tri_gate,
    tri_out,
    bias_v,
    att_proj,
    chain_v,
    same_v,
    att_out,
    proj_t,
    normed,
    tails,
    send_l,
    recv_l,
    send_r,
    recv_r,
    left_m,
    left_t,
    right_m,
    right_t,
    sum_m,
    sum_t,
    send2,
    recv2,
    summed,
    gate,
    mid,
    mid_norm,
    bias_rows,
    send3,
    recv3,
    bias_m,
    bias_tl,
    logit,
    query,
    key,
    value,
    att_gate,
    sends,
    recvs,
):
    me = lax.axis_index("row")

    place = lax.rem(me, NEAR)
    first = me - place

    def other(step):
        return lax.rem(me + step, PARTS)

    def near(step):
        return lax.rem(place + step, NEAR)

    barrier = pltpu.get_barrier_semaphore()

    @pl.loop(1, PARTS)
    def _(step):
        pl.semaphore_signal(
            barrier, inc=1, device_id={"row": other(step)}, device_id_type=pl.DeviceIdType.MESH
        )

    def copy_to(sent, phase, source, landing, slot, part):
        return pltpu.make_async_remote_copy(
            src_ref=source,
            dst_ref=landing.at[slot],
            send_sem=sends.at[sent, part],
            recv_sem=recvs.at[phase, slot],
            device_id={"row": part},
            device_id_type=pl.DeviceIdType.MESH,
        )

    def arrived(phase, landing, slot):
        return pltpu.make_async_remote_copy(
            src_ref=landing.at[slot],
            dst_ref=landing.at[slot],
            send_sem=sends.at[phase, slot],
            recv_sem=recvs.at[phase, slot],
            device_id={"row": other(1)},
            device_id_type=pl.DeviceIdType.MESH,
        )

    def right_copy(part):
        return copy_to(0, 0, send_r.at[lax.rem(part, NEAR)], recv_r, me, part)

    def sum_copy(slot):
        return copy_to(1, 1, send2.at[slot], recv2, place, first + slot)

    def bias_copy(part):
        return copy_to(2, 2, send3, recv3, me, part)

    def left_copy(slot):
        return copy_to(3, 3, send_l.at[slot], recv_l, place, first + slot)

    def passed_copy(slot):
        return copy_to(4, 2, recv3.at[across], recv3, across, first + slot)

    across = lax.rem(me + NEAR, PARTS)

    for fetch in fetches[:3]:
        fetch.wait()

    turned = tri_proj[...].astype(F32).T
    order = [turned[WIDTH * at : WIDTH * at + WIDTH] for at in (1, 3, 0, 2)]
    proj_t[...] = jnp.concatenate(order, axis=0).astype(BF16)
    mask_row = mask_v[...].astype(F32)
    token = lax.broadcasted_iota(jnp.int32, (1, TOKENS), 1)

    def project(i, row, side, send):
        weights = proj_t[2 * WIDTH * side : 2 * WIDTH * side + 2 * WIDTH]
        projected = dot(weights, row, NT)
        mine = jnp.where(token == me * ROWS + i, mask_row, 0.0)
        weight = mask_row * jnp.sum(mine, axis=1, keepdims=True)
        one = weight * jax.nn.sigmoid(projected[WIDTH:]) * projected[:WIDTH]
        send[:, i] = one[:, :128].astype(BF16).reshape(NEAR, SHARE, 128)
        tails[i] = one[:, 128:]

    def pack_tails(send):
        for tile in range(3):
            parts = [tails[i] for i in range(4 * tile, min(4 * tile + 4, ROWS))]
            packed = jnp.concatenate(parts, axis=1)
            if len(parts) < 4:
                packed = pad_lanes(packed)
            send[:, ROWS + tile] = packed.astype(BF16).reshape(NEAR, SHARE, 128)

    @pl.loop(0, ROWS, unroll=2)
    def _(i):
        row = norm(pair[i].astype(F32), 1)
        normed[i] = row
        project(i, row, 0, send_r)

    pack_tails(send_r)
    pl.semaphore_wait(barrier, PARTS - 1)

    @pl.loop(0, NEAR)
    def _(step):
        right_copy(lax.rem(across - place + near(step), PARTS)).start()

    @pl.loop(1, NEAR)
    def _(step):
        right_copy(first + near(step)).start()

    @pl.loop(0, ROWS, unroll=2)
    def _(i):
        project(i, normed[i], 1, send_l)

    pack_tails(send_l)

    @pl.loop(1, NEAR)
    def _(step):
        left_copy(near(step)).start()

    recv_l[place] = send_l[place]
    recv_r[me] = send_r[place]
    for fetch in fetches[3:]:
        fetch.wait()

    @pl.loop(0, ROWS, unroll=5)
    def _(i):
        gate[i] = jax.nn.sigmoid(jnp.dot(normed[i], tri_gate[...], preferred_element_type=F32))

    def unpack(landing, slot, main_f, tail_f):
        for i in range(ROWS):
            at = pl.ds(pl.multiple_of((slot * ROWS + i) * SHARE, SHARE), SHARE)
            main_f[at, :] = landing[slot, i].astype(F32)
            lane = TAIL * (i % 4)
            tail = landing[slot, ROWS + i // 4].astype(F32)[:, lane : lane + TAIL]
            tail_f[at, 0:TAIL] = tail

    @pl.loop(0, NEAR)
    def _(step):
        slot = near(step)

        @pl.when(step > 0)
        def _():
            arrived(3, recv_l, slot).wait_recv()
            arrived(0, recv_r, first + slot).wait_recv()

        unpack(recv_l, slot, left_m, left_t)
        unpack(recv_r, first + slot, right_m, right_t)

    @pl.loop(0, NEAR)
    def _(step):
        source = across - place + near(step)
        arrived(0, recv_r, source).wait_recv()
        unpack(recv_r, source, right_m, right_t)

    for c in range(SHARE):
        at_l, at_r = pl.ds(c, TOKENS // 2, stride=SHARE), pl.ds(c, TOKENS, stride=SHARE)
        main = dot(left_m[at_l, :].astype(BF16), right_m[at_r, :].astype(BF16), NT)
        tail = dot(
            left_t[at_l, :][:, :TAIL].astype(BF16), right_t[at_r, :][:, :TAIL].astype(BF16), NT
        )
        total = main + tail
        sum_m[at_l, :] = total[:, :128]
        sum_t[at_l, :] = pad_lanes(total[:, 128:])

    @pl.loop(0, NEAR)
    def _(step):
        slot = near(step)
        at = pl.ds(pl.multiple_of(slot * ROWS * SHARE, ROWS * SHARE), ROWS * SHARE)
        send2[slot, 0:ROWS] = sum_m[at, :].astype(BF16).reshape(ROWS, SHARE, 128)
        rest = sum_t[at, :][:, :TAIL]
        for tile in range(3):
            parts = [rest[SHARE * i : SHARE * i + SHARE] for i in range(4 * tile, min(4 * tile + 4, ROWS))]
            packed = jnp.concatenate(parts, axis=1)
            if len(parts) < 4:
                packed = pad_lanes(packed)
            send2[slot, ROWS + tile] = packed.astype(BF16)

        @pl.when(step > 0)
        def _():
            sum_copy(slot).start()

    recv2[place] = send2[place]

    @pl.loop(1, NEAR)
    def _(step):
        arrived(1, recv2, near(step)).wait_recv()

    for i in range(ROWS):
        summed[i, :, 0:128] = recv2[:, i].astype(F32).reshape(WIDTH, 128)
        lane = TAIL * (i % 4)
        rest = recv2[:, ROWS + i // 4].astype(F32).reshape(WIDTH, 128)
        summed[i, :, 128:TOKENS] = rest[:, lane : lane + TAIL]

    high = bias_v[...].astype(BF16).astype(F32)
    none = jnp.zeros((HEADS, WIDTH), F32)
    bias_t = jnp.concatenate([high, none, bias_v[...] - high, none], axis=0).astype(BF16)

    @pl.loop(0, ROWS // 2, unroll=5)
    def _(pair_at):
        biases = []
        for half in range(2):
            i = pair_at * 2 + half
            tri_norm = norm(summed[i], 0)
            update = dot(tri_norm, tri_out[...], TN)
            mid_row = (pair[i].astype(F32) + gate[i] * update).astype(BF16)
            mid[i] = mid_row
            mid_n = norm(mid_row.astype(F32), 1)
            mid_norm[i] = mid_n
            bias = dot(bias_t, mid_n, NT)
            biases.append(bias[0:8] + bias[8:16])
        joined = jnp.concatenate([biases[0][0:HEADS], biases[1][0:HEADS]], axis=0)
        bias_rows[pl.ds(pl.multiple_of(pair_at * 8, 8), 8), :] = joined

    send3[0:32] = bias_rows[0:32, 0:128].astype(BF16)
    send3[32:48] = jnp.concatenate(
        [bias_rows[32:40, 0:128], jnp.zeros((8, 128), F32)], axis=0
    ).astype(BF16)
    last = jnp.concatenate([bias_rows[32:40, 128:TOKENS], jnp.zeros((8, TAIL), F32)], axis=0)
    send3[48:64] = pad_lanes(
        jnp.concatenate(
            [bias_rows[0:16, 128:TOKENS], bias_rows[16:32, 128:TOKENS], last], axis=1
        )
    ).astype(BF16)

    bias_copy(across).start()

    @pl.loop(1, NEAR)
    def _(step):
        bias_copy(first + near(step)).start()

    recv3[me] = send3[...]

    query_t = att_proj[:, 0:WIDTH].astype(F32).T.astype(BF16)
    channel = lax.broadcasted_iota(jnp.int32, (WIDTH, HEADS * TOKENS), 0) // (WIDTH // HEADS)
    lane = lax.broadcasted_iota(jnp.int32, (WIDTH, HEADS * TOKENS), 1)
    block = (lane >= channel * TOKENS) & (lane < channel * TOKENS + TOKENS)
    scale = (WIDTH // HEADS) ** (-0.5)

    def attention_inputs(i):
        mid_n = mid_norm[i]
        rest = jnp.dot(mid_n, att_proj[:, WIDTH:], preferred_element_type=F32)
        key[i] = rest[:, 0:WIDTH].astype(BF16)
        value[i] = rest[:, WIDTH : 2 * WIDTH].astype(BF16)
        att_gate[i] = jax.nn.sigmoid(rest[:, 2 * WIDTH :])
        wide = dot(query_t, jnp.concatenate([mid_n] * HEADS, axis=0), NT)
        query[i] = jnp.where(block, wide * scale, 0.0).astype(BF16)

    pl.loop(0, EARLY, unroll=5)(attention_inputs)
    arrived(2, recv3, across).wait_recv()

    @pl.loop(1, NEAR)
    def _(step):
        passed_copy(near(step)).start()

    pl.loop(EARLY, ROWS, unroll=5)(attention_inputs)

    ids = lax.broadcasted_iota(jnp.int32, (16, TOKENS), 0)
    one_hot = jnp.where(ids == chain_v[...], 1.0, 0.0).astype(BF16)
    same = dot(one_hot, one_hot, TN)
    absent = 10000.0 * (mask_row - 1.0)

    @pl.loop(0, PARTS)
    def _(step):
        source = other(step)

        @pl.when((step > 0) & (step != NEAR))
        def _():
            arrived(2, recv3, source).wait_recv()

        at = pl.multiple_of(source * 40, 8)
        got = recv3[source].astype(F32)
        bias_m[pl.ds(at, 40), :] = got[0:40]
        for t in range(3):
            size = 16 if t < 2 else 8
            bias_tl[pl.ds(pl.multiple_of(at + 16 * t, 8), size), 0:TAIL] = got[
                48 : 48 + size, TAIL * t : TAIL * t + TAIL
            ]

    mains, rests = [], []
    for h in range(HEADS):
        extra = same_v[0:1, h : h + 1] * same
        every = pl.ds(h, TOKENS, stride=HEADS)
        mains.append(bias_m[every, :] + extra[:, 0:128] + absent[:, 0:128])
        rest = bias_tl[every, :][:, :TAIL] + extra[:, 128:] + absent[:, 128:]
        rests.append(pad_lanes(rest))
    logit[0:128, :] = jnp.concatenate(mains, axis=0).T
    logit[128:TOKENS, :] = jnp.concatenate(rests, axis=0).T[0:TAIL]

    head_of = lax.broadcasted_iota(jnp.int32, (TOKENS, WIDTH), 1) // (WIDTH // HEADS)

    @pl.loop(0, ROWS, unroll=5)
    def _(i):
        scores = jnp.dot(key[i], query[i], preferred_element_type=F32) + logit[...]
        top = jnp.max(scores, axis=0, keepdims=True)
        exps = jnp.exp(scores - top)
        weight = (exps * (1.0 / jnp.sum(exps, axis=0, keepdims=True))).astype(BF16)
        mixes = dot(weight, value[i], TN)
        mixed = mixes[0:TOKENS]
        for h in range(1, HEADS):
            mixed = jnp.where(head_of == h, mixes[h * TOKENS : (h + 1) * TOKENS], mixed)
        gated = (att_gate[i] * mixed).astype(BF16)
        added = jnp.dot(gated, att_out[...], preferred_element_type=F32)
        out[i] = (mid[i].astype(F32) + added).astype(BF16)

    @pl.loop(1, PARTS)
    def _(step):
        right_copy(other(step)).wait_send()

    bias_copy(across).wait_send()

    @pl.loop(1, NEAR)
    def _(step):
        slot = near(step)
        left_copy(slot).wait_send()
        sum_copy(slot).wait_send()
        bias_copy(first + slot).wait_send()
        passed_copy(slot).wait_send()


def per_device_fused(
    pair, mask, chain, tri_proj, tri_gate, tri_out, att_proj, att_bias, same_chain, att_out
):
    hbm = pl.BlockSpec(memory_space=pltpu.HBM)
    vmem = pl.BlockSpec(memory_space=pltpu.VMEM)
    all_rows = (ROWS, TOKENS, WIDTH)
    inputs = (
        pair,
        tri_proj,
        mask.reshape(1, TOKENS),
        tri_gate,
        tri_out,
        att_bias.T,
        att_proj,
        chain.reshape(1, TOKENS),
        same_chain.reshape(1, HEADS),
        att_out,
    )
    return pl.pallas_call(
        fused_kernel,
        out_shape=jax.ShapeDtypeStruct(all_rows, BF16),
        in_specs=[hbm] * 10,
        out_specs=vmem,
        scratch_shapes=[pltpu.VMEM(each.shape, each.dtype) for each in inputs]
        + [
            pltpu.VMEM((4 * WIDTH, WIDTH), BF16),
            pltpu.VMEM(all_rows, BF16),
            pltpu.VMEM((ROWS, WIDTH, TAIL), F32),
            pltpu.VMEM((NEAR, TILES, SHARE, 128), BF16),
            pltpu.VMEM((NEAR, TILES, SHARE, 128), BF16),
            pltpu.VMEM((NEAR, TILES, SHARE, 128), BF16),
            pltpu.VMEM((PARTS, TILES, SHARE, 128), BF16),
            pltpu.VMEM((TOKENS // 2 * SHARE, 128), F32),
            pltpu.VMEM((TOKENS // 2 * SHARE, 128), F32),
            pltpu.VMEM((TOKENS * SHARE, 128), F32),
            pltpu.VMEM((TOKENS * SHARE, 128), F32),
            pltpu.VMEM((TOKENS // 2 * SHARE, 128), F32),
            pltpu.VMEM((TOKENS // 2 * SHARE, 128), F32),
            pltpu.VMEM((NEAR, TILES, SHARE, 128), BF16),
            pltpu.VMEM((NEAR, TILES, SHARE, 128), BF16),
            pltpu.VMEM((ROWS, WIDTH, TOKENS), F32),
            pltpu.VMEM(all_rows, F32),
            pltpu.VMEM(all_rows, BF16),
            pltpu.VMEM(all_rows, BF16),
            pltpu.VMEM((40, TOKENS), F32),
            pltpu.VMEM((64, 128), BF16),
            pltpu.VMEM((PARTS, 64, 128), BF16),
            pltpu.VMEM((TOKENS * HEADS, 128), F32),
            pltpu.VMEM((TOKENS * HEADS, 128), F32),
            pltpu.VMEM((TOKENS, HEADS * TOKENS), F32),
            pltpu.VMEM((ROWS, WIDTH, HEADS * TOKENS), BF16),
            pltpu.VMEM(all_rows, BF16),
            pltpu.VMEM(all_rows, BF16),
            pltpu.VMEM(all_rows, F32),
            pltpu.SemaphoreType.DMA((5, PARTS)),
            pltpu.SemaphoreType.DMA((5, PARTS)),
            pltpu.SemaphoreType.DMA((10,)),
        ],
        compiler_params=pltpu.CompilerParams(
            collective_id=0, has_side_effects=True, vmem_limit_bytes=64 * 1024 * 1024
        ),
    )(*inputs)


def per_device(pair, *others):
    fits = pair.shape == (ROWS, TOKENS, WIDTH) and lax.axis_size("row") == PARTS
    return (per_device_fused if fits else per_device_general)(pair, *others)


def solution(mesh):
    return jax.shard_map(
        per_device,
        mesh=mesh,
        in_specs=(
            P(("groups", "row"), None, None),
            P("groups"),
            P("groups"),
            P(),
            P(),
            P(),
            P(),
            P(),
            P(),
            P(),
        ),
        out_specs=P(("groups", "row"), None, None),
        check_vma=False,
    )
```

```python
import jax
import jax.numpy as jnp
from jax import lax
from jax.experimental import pallas as pl
from jax.experimental.pallas import tpu as pltpu
from jax.sharding import PartitionSpec as P

F32 = jnp.float32
BF16 = jnp.bfloat16
NT = (((1,), (1,)), ((), ()))
TN = (((0,), (0,)), ((), ()))


def layer_norm(values):
    centre_mean = jnp.mean(values, axis=-1, keepdims=True)
    centred = values - centre_mean
    spread = jnp.mean(centred * centred, axis=-1, keepdims=True)
    return centred * lax.rsqrt(spread + 1e-05)


def chain_logits(bias_block, same_chain, chain_rows, chain, mask_float):
    same = (chain_rows[:, None] == chain[None, :]).astype(jnp.float32)
    logit_bias = bias_block.astype(jnp.float32) + same_chain[:, None, None] * same[None, :, :]
    return logit_bias + 10000.0 * (mask_float - 1.0)[None, None, :]


def attend(query, att_gate, key, value, logit_bias, head_count, head_size):
    block_len = query.shape[1]
    tokens = key.shape[1]
    width = head_count * head_size

    def one_row(inputs):
        query_row, key_row, value_row, gate_row = inputs
        query_heads = query_row.reshape(block_len, head_count, head_size)
        key_heads = key_row.reshape(tokens, head_count, head_size)
        value_heads = value_row.reshape(tokens, head_count, head_size)
        scores = (
            jnp.einsum("jhd,khd->hjk", query_heads, key_heads, preferred_element_type=jnp.float32)
            + logit_bias
        )
        row_max = jnp.max(scores, axis=2, keepdims=True)
        exp_scores = jnp.exp(scores - row_max)
        weight = (exp_scores / jnp.sum(exp_scores, axis=2, keepdims=True)).astype(jnp.bfloat16)
        mixed_heads = jnp.einsum(
            "hjk,khd->jhd", weight, value_heads, preferred_element_type=jnp.float32
        )
        return (gate_row * mixed_heads.reshape(block_len, width)).astype(jnp.bfloat16)

    return lax.map(one_row, (query, key, value, att_gate))


def per_device_general(
    pair, mask, chain, tri_proj, tri_gate, tri_out, att_proj, att_bias, same_chain, att_out
):
    local_rows, tokens, width = pair.shape
    head_count = same_chain.shape[0]
    head_size = width // head_count
    scale = head_size ** (-0.5)
    part_count = lax.axis_size("row")
    share_width = width // part_count
    first_row = lax.axis_index("row") * local_rows
    mask_float = mask.astype(jnp.float32)
    row_mask = lax.dynamic_slice_in_dim(mask_float, first_row, local_rows)

    def project_row(inputs):
        pair_row, mask_value = inputs
        normed = layer_norm(pair_row.astype(jnp.float32)).astype(jnp.bfloat16)
        projected = jnp.dot(normed, tri_proj, preferred_element_type=jnp.float32)
        weight = (mask_value * mask_float)[:, None]
        left_proj = (
            weight * jax.nn.sigmoid(projected[:, 2 * width : 3 * width]) * projected[:, :width]
        ).astype(jnp.bfloat16)
        right_proj = (
            weight * jax.nn.sigmoid(projected[:, 3 * width :]) * projected[:, width : 2 * width]
        ).astype(jnp.bfloat16)
        out_gate = jax.nn.sigmoid(jnp.dot(normed, tri_gate, preferred_element_type=jnp.float32))
        return (left_proj, right_proj, out_gate)

    left_proj, right_proj, out_gate = lax.map(project_row, (pair, row_mask))
    left_lay = jnp.transpose(left_proj, (2, 0, 1)).reshape(
        part_count, share_width, local_rows, tokens
    )
    right_lay = jnp.transpose(right_proj, (2, 0, 1)).reshape(
        part_count, share_width, local_rows, tokens
    )
    got_left, got_right = (
        lax.all_to_all(left_lay, "row", split_axis=0, concat_axis=2, tiled=True),
        lax.all_to_all(right_lay, "row", split_axis=0, concat_axis=2, tiled=True),
    )
    product = jnp.einsum(
        "cik,cjk->cij", got_left[0], got_right[0], preferred_element_type=jnp.float32
    )
    returned = lax.all_to_all(
        product.astype(jnp.bfloat16)[None], "row", split_axis=2, concat_axis=0, tiled=True
    )
    tri_sum = jnp.transpose(returned.reshape(width, local_rows, tokens), (1, 2, 0))

    def finish_row(inputs):
        pair_row, summed, gate_row = inputs
        tri_norm = layer_norm(summed.astype(jnp.float32)).astype(jnp.bfloat16)
        update = jnp.dot(tri_norm, tri_out, preferred_element_type=jnp.float32)
        mid_pair = (pair_row.astype(jnp.float32) + gate_row * update).astype(jnp.bfloat16)
        mid_norm = layer_norm(mid_pair.astype(jnp.float32)).astype(jnp.bfloat16)
        att_all = jnp.dot(mid_norm, att_proj, preferred_element_type=jnp.float32)
        query = (att_all[:, :width] * scale).astype(jnp.bfloat16)
        key = att_all[:, width : 2 * width].astype(jnp.bfloat16)
        value = att_all[:, 2 * width : 3 * width].astype(jnp.bfloat16)
        att_gate = jax.nn.sigmoid(att_all[:, 3 * width :])
        pair_bias = jnp.dot(mid_norm, att_bias, preferred_element_type=jnp.float32).astype(
            jnp.bfloat16
        )
        return (mid_pair, query, key, value, att_gate, pair_bias)

    mid_pair, query, key, value, att_gate, pair_bias = lax.map(
        finish_row, (pair, tri_sum, out_gate)
    )
    bias_lay = jnp.transpose(pair_bias, (2, 0, 1))
    full_bias = lax.all_gather(bias_lay, "row", axis=1, tiled=True)
    logit_bias = chain_logits(full_bias, same_chain, chain, chain, mask_float)
    gated = attend(query, att_gate, key, value, logit_bias, head_count, head_size)
    projected_out = jnp.dot(gated.reshape(-1, width), att_out, preferred_element_type=jnp.float32)
    return (mid_pair.astype(jnp.float32) + projected_out.reshape(local_rows, tokens, width)).astype(
        jnp.bfloat16
    )


ROWS, TOKENS, WIDTH, PARTS, HEADS = 10, 160, 128, 16, 4
NEAR = PARTS // 2
SHARE = WIDTH // NEAR
TILES = 13
EARLY = 5
TAIL = TOKENS - 128


def dot(left, right, dims):
    return lax.dot_general(left, right, dims, preferred_element_type=F32)


def norm(values, axis):
    centred = values - jnp.mean(values, axis=axis, keepdims=True)
    spread = jnp.mean(centred * centred, axis=axis, keepdims=True)
    return (centred * lax.rsqrt(spread + 1e-05)).astype(BF16)


def pad_lanes(values):
    return jnp.concatenate(
        [values, jnp.zeros((values.shape[0], 128 - values.shape[1]), values.dtype)], axis=1
    )


def fused_kernel(
    *refs,
):
    outside, (out, *inside, loads) = refs[:10], refs[10:]
    held, scratch = inside[:10], inside[10:]
    fetches = [
        pltpu.make_async_copy(source, target, loads.at[k])
        for k, (source, target) in enumerate(zip(outside, held))
    ]
    for fetch in fetches:
        fetch.start()
    fused_body(fetches, out, *held, *scratch)


def fused_body(
    fetches,
    out,
    pair,
    tri_proj,
    mask_v,
    tri_gate,
    tri_out,
    bias_v,
    att_proj,
    chain_v,
    same_v,
    att_out,
    proj_t,
    normed,
    tails,
    send_l,
    recv_l,
    send_r,
    recv_r,
    left_m,
    left_t,
    right_m,
    right_t,
    sum_m,
    sum_t,
    send2,
    recv2,
    summed,
    gate,
    mid,
    mid_norm,
    bias_rows,
    send3,
    recv3,
    bias_m,
    bias_tl,
    logit,
    query,
    key,
    value,
    att_gate,
    sends,
    recvs,
    stores,
):
    me = lax.axis_index("row")

    place = lax.rem(me, NEAR)
    first = me - place

    def other(step):
        return lax.rem(me + step, PARTS)

    def near(step):
        return lax.rem(place + step, NEAR)

    barrier = pltpu.get_barrier_semaphore()

    @pl.loop(1, PARTS)
    def _(step):
        pl.semaphore_signal(
            barrier, inc=1, device_id={"row": other(step)}, device_id_type=pl.DeviceIdType.MESH
        )

    def copy_to(sent, phase, source, landing, slot, part):
        return pltpu.make_async_remote_copy(
            src_ref=source,
            dst_ref=landing.at[slot],
            send_sem=sends.at[sent, part],
            recv_sem=recvs.at[phase, slot],
            device_id={"row": part},
            device_id_type=pl.DeviceIdType.MESH,
        )

    def arrived(phase, landing, slot):
        return pltpu.make_async_remote_copy(
            src_ref=landing.at[slot],
            dst_ref=landing.at[slot],
            send_sem=sends.at[phase, slot],
            recv_sem=recvs.at[phase, slot],
            device_id={"row": other(1)},
            device_id_type=pl.DeviceIdType.MESH,
        )

    def right_copy(part):
        return copy_to(0, 0, send_r.at[lax.rem(part, NEAR)], recv_r, me, part)

    def sum_copy(slot):
        return copy_to(1, 1, send2.at[slot], recv2, place, first + slot)

    def bias_copy(part):
        return copy_to(2, 2, send3, recv3, me, part)

    def left_copy(slot):
        return copy_to(3, 3, send_l.at[slot], recv_l, place, first + slot)

    def passed_copy(slot):
        return copy_to(4, 2, recv3.at[across], recv3, across, first + slot)

    across = lax.rem(me + NEAR, PARTS)

    for fetch in fetches[:3]:
        fetch.wait()

    turned = tri_proj[...].astype(F32).T
    order = [turned[WIDTH * at : WIDTH * at + WIDTH] for at in (1, 3, 0, 2)]
    proj_t[...] = jnp.concatenate(order, axis=0).astype(BF16)
    mask_row = mask_v[...].astype(F32)
    token = lax.broadcasted_iota(jnp.int32, (1, TOKENS), 1)

    def project(i, row, side, send):
        weights = proj_t[2 * WIDTH * side : 2 * WIDTH * side + 2 * WIDTH]
        projected = dot(weights, row, NT)
        mine = jnp.where(token == me * ROWS + i, mask_row, 0.0)
        weight = mask_row * jnp.sum(mine, axis=1, keepdims=True)
        one = weight * jax.nn.sigmoid(projected[WIDTH:]) * projected[:WIDTH]
        send[:, i] = one[:, :128].astype(BF16).reshape(NEAR, SHARE, 128)
        tails[i] = one[:, 128:]

    def pack_tails(send):
        for tile in range(3):
            parts = [tails[i] for i in range(4 * tile, min(4 * tile + 4, ROWS))]
            packed = jnp.concatenate(parts, axis=1)
            if len(parts) < 4:
                packed = pad_lanes(packed)
            send[:, ROWS + tile] = packed.astype(BF16).reshape(NEAR, SHARE, 128)

    @pl.loop(0, ROWS, unroll=2)
    def _(i):
        row = norm(pair[i].astype(F32), 1)
        normed[i] = row
        project(i, row, 0, send_r)

    pack_tails(send_r)
    pl.semaphore_wait(barrier, PARTS - 1)

    @pl.loop(0, NEAR)
    def _(step):
        right_copy(lax.rem(across - place + near(step), PARTS)).start()

    @pl.loop(1, NEAR)
    def _(step):
        right_copy(first + near(step)).start()

    @pl.loop(0, ROWS, unroll=2)
    def _(i):
        project(i, normed[i], 1, send_l)

    pack_tails(send_l)

    @pl.loop(1, NEAR)
    def _(step):
        left_copy(near(step)).start()

    recv_l[place] = send_l[place]
    recv_r[me] = send_r[place]
    for fetch in fetches[3:]:
        fetch.wait()

    @pl.loop(0, ROWS, unroll=5)
    def _(i):
        gate[i] = jax.nn.sigmoid(jnp.dot(normed[i], tri_gate[...], preferred_element_type=F32))

    def unpack(landing, slot, main_f, tail_f):
        for i in range(ROWS):
            at = pl.ds(pl.multiple_of((slot * ROWS + i) * SHARE, SHARE), SHARE)
            main_f[at, :] = landing[slot, i].astype(F32)
            lane = TAIL * (i % 4)
            tail = landing[slot, ROWS + i // 4].astype(F32)[:, lane : lane + TAIL]
            tail_f[at, 0:TAIL] = tail

    @pl.loop(0, NEAR)
    def _(step):
        slot = near(step)

        @pl.when(step > 0)
        def _():
            arrived(3, recv_l, slot).wait_recv()
            arrived(0, recv_r, first + slot).wait_recv()

        unpack(recv_l, slot, left_m, left_t)
        unpack(recv_r, first + slot, right_m, right_t)

    @pl.loop(0, NEAR)
    def _(step):
        source = across - place + near(step)
        arrived(0, recv_r, source).wait_recv()
        unpack(recv_r, source, right_m, right_t)

    for c in range(SHARE):
        at_l, at_r = pl.ds(c, TOKENS // 2, stride=SHARE), pl.ds(c, TOKENS, stride=SHARE)
        main = dot(left_m[at_l, :].astype(BF16), right_m[at_r, :].astype(BF16), NT)
        tail = dot(
            left_t[at_l, :][:, :TAIL].astype(BF16), right_t[at_r, :][:, :TAIL].astype(BF16), NT
        )
        total = main + tail
        sum_m[at_l, :] = total[:, :128]
        sum_t[at_l, :] = pad_lanes(total[:, 128:])

    @pl.loop(0, NEAR)
    def _(step):
        slot = near(step)
        at = pl.ds(pl.multiple_of(slot * ROWS * SHARE, ROWS * SHARE), ROWS * SHARE)
        send2[slot, 0:ROWS] = sum_m[at, :].astype(BF16).reshape(ROWS, SHARE, 128)
        rest = sum_t[at, :][:, :TAIL]
        for tile in range(3):
            parts = [rest[SHARE * i : SHARE * i + SHARE] for i in range(4 * tile, min(4 * tile + 4, ROWS))]
            packed = jnp.concatenate(parts, axis=1)
            if len(parts) < 4:
                packed = pad_lanes(packed)
            send2[slot, ROWS + tile] = packed.astype(BF16)

        @pl.when(step > 0)
        def _():
            sum_copy(slot).start()

    recv2[place] = send2[place]

    @pl.loop(1, NEAR)
    def _(step):
        arrived(1, recv2, near(step)).wait_recv()

    for i in range(ROWS):
        summed[i, :, 0:128] = recv2[:, i].astype(F32).reshape(WIDTH, 128)
        lane = TAIL * (i % 4)
        rest = recv2[:, ROWS + i // 4].astype(F32).reshape(WIDTH, 128)
        summed[i, :, 128:TOKENS] = rest[:, lane : lane + TAIL]

    high = bias_v[...].astype(BF16).astype(F32)
    none = jnp.zeros((HEADS, WIDTH), F32)
    bias_t = jnp.concatenate([high, none, bias_v[...] - high, none], axis=0).astype(BF16)

    @pl.loop(0, ROWS // 2, unroll=5)
    def _(pair_at):
        biases = []
        for half in range(2):
            i = pair_at * 2 + half
            tri_norm = norm(summed[i], 0)
            update = dot(tri_norm, tri_out[...], TN)
            mid_row = (pair[i].astype(F32) + gate[i] * update).astype(BF16)
            mid[i] = mid_row
            mid_n = norm(mid_row.astype(F32), 1)
            mid_norm[i] = mid_n
            bias = dot(bias_t, mid_n, NT)
            biases.append(bias[0:8] + bias[8:16])
        joined = jnp.concatenate([biases[0][0:HEADS], biases[1][0:HEADS]], axis=0)
        bias_rows[pl.ds(pl.multiple_of(pair_at * 8, 8), 8), :] = joined

    send3[0:32] = bias_rows[0:32, 0:128].astype(BF16)
    send3[32:48] = jnp.concatenate(
        [bias_rows[32:40, 0:128], jnp.zeros((8, 128), F32)], axis=0
    ).astype(BF16)
    last = jnp.concatenate([bias_rows[32:40, 128:TOKENS], jnp.zeros((8, TAIL), F32)], axis=0)
    send3[48:64] = pad_lanes(
        jnp.concatenate(
            [bias_rows[0:16, 128:TOKENS], bias_rows[16:32, 128:TOKENS], last], axis=1
        )
    ).astype(BF16)

    bias_copy(across).start()

    @pl.loop(1, NEAR)
    def _(step):
        bias_copy(first + near(step)).start()

    recv3[me] = send3[...]

    query_t = att_proj[:, 0:WIDTH].astype(F32).T.astype(BF16)
    channel = lax.broadcasted_iota(jnp.int32, (WIDTH, HEADS * TOKENS), 0) // (WIDTH // HEADS)
    lane = lax.broadcasted_iota(jnp.int32, (WIDTH, HEADS * TOKENS), 1)
    block = (lane >= channel * TOKENS) & (lane < channel * TOKENS + TOKENS)
    scale = (WIDTH // HEADS) ** (-0.5)

    def attention_inputs(i):
        mid_n = mid_norm[i]
        rest = jnp.dot(mid_n, att_proj[:, WIDTH:], preferred_element_type=F32)
        key[i] = rest[:, 0:WIDTH].astype(BF16)
        value[i] = rest[:, WIDTH : 2 * WIDTH].astype(BF16)
        att_gate[i] = jax.nn.sigmoid(rest[:, 2 * WIDTH :])
        wide = dot(query_t, jnp.concatenate([mid_n] * HEADS, axis=0), NT)
        query[i] = jnp.where(block, wide * scale, 0.0).astype(BF16)

    pl.loop(0, EARLY, unroll=5)(attention_inputs)
    arrived(2, recv3, across).wait_recv()

    @pl.loop(1, NEAR)
    def _(step):
        passed_copy(near(step)).start()

    pl.loop(EARLY, ROWS, unroll=5)(attention_inputs)

    ids = lax.broadcasted_iota(jnp.int32, (16, TOKENS), 0)
    one_hot = jnp.where(ids == chain_v[...], 1.0, 0.0).astype(BF16)
    same = dot(one_hot, one_hot, TN)
    absent = 10000.0 * (mask_row - 1.0)

    @pl.loop(0, PARTS)
    def _(step):
        source = other(step)

        @pl.when((step > 0) & (step != NEAR))
        def _():
            arrived(2, recv3, source).wait_recv()

        at = pl.multiple_of(source * 40, 8)
        got = recv3[source].astype(F32)
        bias_m[pl.ds(at, 40), :] = got[0:40]
        for t in range(3):
            size = 16 if t < 2 else 8
            bias_tl[pl.ds(pl.multiple_of(at + 16 * t, 8), size), 0:TAIL] = got[
                48 : 48 + size, TAIL * t : TAIL * t + TAIL
            ]

    mains, rests = [], []
    for h in range(HEADS):
        extra = same_v[0:1, h : h + 1] * same
        every = pl.ds(h, TOKENS, stride=HEADS)
        mains.append(bias_m[every, :] + extra[:, 0:128] + absent[:, 0:128])
        rest = bias_tl[every, :][:, :TAIL] + extra[:, 128:] + absent[:, 128:]
        rests.append(pad_lanes(rest))
    logit[0:128, :] = jnp.concatenate(mains, axis=0).T
    logit[128:TOKENS, :] = jnp.concatenate(rests, axis=0).T[0:TAIL]

    def row_out(i):
        return pltpu.make_async_copy(mid.at[i], out.at[i], stores.at[i])

    head_of = lax.broadcasted_iota(jnp.int32, (TOKENS, WIDTH), 1) // (WIDTH // HEADS)

    @pl.loop(0, ROWS, unroll=5)
    def _(i):
        scores = jnp.dot(key[i], query[i], preferred_element_type=F32) + logit[...]
        top = jnp.max(scores, axis=0, keepdims=True)
        exps = jnp.exp(scores - top)
        weight = (exps * (1.0 / jnp.sum(exps, axis=0, keepdims=True))).astype(BF16)
        mixes = dot(weight, value[i], TN)
        mixed = mixes[0:TOKENS]
        for h in range(1, HEADS):
            mixed = jnp.where(head_of == h, mixes[h * TOKENS : (h + 1) * TOKENS], mixed)
        gated = (att_gate[i] * mixed).astype(BF16)
        added = jnp.dot(gated, att_out[...], preferred_element_type=F32)
        mid[i] = (mid[i].astype(F32) + added).astype(BF16)
        row_out(i).start()

    @pl.loop(1, PARTS)
    def _(step):
        right_copy(other(step)).wait_send()

    bias_copy(across).wait_send()

    @pl.loop(0, ROWS)
    def _(i):
        row_out(i).wait()

    @pl.loop(1, NEAR)
    def _(step):
        slot = near(step)
        left_copy(slot).wait_send()
        sum_copy(slot).wait_send()
        bias_copy(first + slot).wait_send()
        passed_copy(slot).wait_send()


def per_device_fused(
    pair, mask, chain, tri_proj, tri_gate, tri_out, att_proj, att_bias, same_chain, att_out
):
    hbm = pl.BlockSpec(memory_space=pltpu.HBM)
    all_rows = (ROWS, TOKENS, WIDTH)
    inputs = (
        pair,
        tri_proj,
        mask.reshape(1, TOKENS),
        tri_gate,
        tri_out,
        att_bias.T,
        att_proj,
        chain.reshape(1, TOKENS),
        same_chain.reshape(1, HEADS),
        att_out,
    )
    return pl.pallas_call(
        fused_kernel,
        out_shape=jax.ShapeDtypeStruct(all_rows, BF16),
        in_specs=[hbm] * 10,
        out_specs=hbm,
        scratch_shapes=[pltpu.VMEM(each.shape, each.dtype) for each in inputs]
        + [
            pltpu.VMEM((4 * WIDTH, WIDTH), BF16),
            pltpu.VMEM(all_rows, BF16),
            pltpu.VMEM((ROWS, WIDTH, TAIL), F32),
            pltpu.VMEM((NEAR, TILES, SHARE, 128), BF16),
            pltpu.VMEM((NEAR, TILES, SHARE, 128), BF16),
            pltpu.VMEM((NEAR, TILES, SHARE, 128), BF16),
            pltpu.VMEM((PARTS, TILES, SHARE, 128), BF16),
            pltpu.VMEM((TOKENS // 2 * SHARE, 128), F32),
            pltpu.VMEM((TOKENS // 2 * SHARE, 128), F32),
            pltpu.VMEM((TOKENS * SHARE, 128), F32),
            pltpu.VMEM((TOKENS * SHARE, 128), F32),
            pltpu.VMEM((TOKENS // 2 * SHARE, 128), F32),
            pltpu.VMEM((TOKENS // 2 * SHARE, 128), F32),
            pltpu.VMEM((NEAR, TILES, SHARE, 128), BF16),
            pltpu.VMEM((NEAR, TILES, SHARE, 128), BF16),
            pltpu.VMEM((ROWS, WIDTH, TOKENS), F32),
            pltpu.VMEM(all_rows, F32),
            pltpu.VMEM(all_rows, BF16),
            pltpu.VMEM(all_rows, BF16),
            pltpu.VMEM((40, TOKENS), F32),
            pltpu.VMEM((64, 128), BF16),
            pltpu.VMEM((PARTS, 64, 128), BF16),
            pltpu.VMEM((TOKENS * HEADS, 128), F32),
            pltpu.VMEM((TOKENS * HEADS, 128), F32),
            pltpu.VMEM((TOKENS, HEADS * TOKENS), F32),
            pltpu.VMEM((ROWS, WIDTH, HEADS * TOKENS), BF16),
            pltpu.VMEM(all_rows, BF16),
            pltpu.VMEM(all_rows, BF16),
            pltpu.VMEM(all_rows, F32),
            pltpu.SemaphoreType.DMA((5, PARTS)),
            pltpu.SemaphoreType.DMA((5, PARTS)),
            pltpu.SemaphoreType.DMA((ROWS,)),
            pltpu.SemaphoreType.DMA((10,)),
        ],
        compiler_params=pltpu.CompilerParams(
            collective_id=0, has_side_effects=True, vmem_limit_bytes=64 * 1024 * 1024
        ),
    )(*inputs)


def per_device(pair, *others):
    fits = pair.shape == (ROWS, TOKENS, WIDTH) and lax.axis_size("row") == PARTS
    return (per_device_fused if fits else per_device_general)(pair, *others)


def solution(mesh):
    return jax.shard_map(
        per_device,
        mesh=mesh,
        in_specs=(
            P(("groups", "row"), None, None),
            P("groups"),
            P("groups"),
            P(),
            P(),
            P(),
            P(),
            P(),
            P(),
            P(),
        ),
        out_specs=P(("groups", "row"), None, None),
        check_vma=False,
    )
```

```python
import jax
import jax.numpy as jnp
from jax import lax
from jax.experimental import pallas as pl
from jax.experimental.pallas import tpu as pltpu
from jax.sharding import PartitionSpec as P

F32 = jnp.float32
BF16 = jnp.bfloat16
NT = (((1,), (1,)), ((), ()))
TN = (((0,), (0,)), ((), ()))


def layer_norm(values):
    centre_mean = jnp.mean(values, axis=-1, keepdims=True)
    centred = values - centre_mean
    spread = jnp.mean(centred * centred, axis=-1, keepdims=True)
    return centred * lax.rsqrt(spread + 1e-05)


def chain_logits(bias_block, same_chain, chain_rows, chain, mask_float):
    same = (chain_rows[:, None] == chain[None, :]).astype(jnp.float32)
    logit_bias = bias_block.astype(jnp.float32) + same_chain[:, None, None] * same[None, :, :]
    return logit_bias + 10000.0 * (mask_float - 1.0)[None, None, :]


def attend(query, att_gate, key, value, logit_bias, head_count, head_size):
    block_len = query.shape[1]
    tokens = key.shape[1]
    width = head_count * head_size

    def one_row(inputs):
        query_row, key_row, value_row, gate_row = inputs
        query_heads = query_row.reshape(block_len, head_count, head_size)
        key_heads = key_row.reshape(tokens, head_count, head_size)
        value_heads = value_row.reshape(tokens, head_count, head_size)
        scores = (
            jnp.einsum("jhd,khd->hjk", query_heads, key_heads, preferred_element_type=jnp.float32)
            + logit_bias
        )
        row_max = jnp.max(scores, axis=2, keepdims=True)
        exp_scores = jnp.exp(scores - row_max)
        weight = (exp_scores / jnp.sum(exp_scores, axis=2, keepdims=True)).astype(jnp.bfloat16)
        mixed_heads = jnp.einsum(
            "hjk,khd->jhd", weight, value_heads, preferred_element_type=jnp.float32
        )
        return (gate_row * mixed_heads.reshape(block_len, width)).astype(jnp.bfloat16)

    return lax.map(one_row, (query, key, value, att_gate))


def per_device_general(
    pair, mask, chain, tri_proj, tri_gate, tri_out, att_proj, att_bias, same_chain, att_out
):
    local_rows, tokens, width = pair.shape
    head_count = same_chain.shape[0]
    head_size = width // head_count
    scale = head_size ** (-0.5)
    part_count = lax.axis_size("row")
    share_width = width // part_count
    first_row = lax.axis_index("row") * local_rows
    mask_float = mask.astype(jnp.float32)
    row_mask = lax.dynamic_slice_in_dim(mask_float, first_row, local_rows)

    def project_row(inputs):
        pair_row, mask_value = inputs
        normed = layer_norm(pair_row.astype(jnp.float32)).astype(jnp.bfloat16)
        projected = jnp.dot(normed, tri_proj, preferred_element_type=jnp.float32)
        weight = (mask_value * mask_float)[:, None]
        left_proj = (
            weight * jax.nn.sigmoid(projected[:, 2 * width : 3 * width]) * projected[:, :width]
        ).astype(jnp.bfloat16)
        right_proj = (
            weight * jax.nn.sigmoid(projected[:, 3 * width :]) * projected[:, width : 2 * width]
        ).astype(jnp.bfloat16)
        out_gate = jax.nn.sigmoid(jnp.dot(normed, tri_gate, preferred_element_type=jnp.float32))
        return (left_proj, right_proj, out_gate)

    left_proj, right_proj, out_gate = lax.map(project_row, (pair, row_mask))
    left_lay = jnp.transpose(left_proj, (2, 0, 1)).reshape(
        part_count, share_width, local_rows, tokens
    )
    right_lay = jnp.transpose(right_proj, (2, 0, 1)).reshape(
        part_count, share_width, local_rows, tokens
    )
    got_left, got_right = (
        lax.all_to_all(left_lay, "row", split_axis=0, concat_axis=2, tiled=True),
        lax.all_to_all(right_lay, "row", split_axis=0, concat_axis=2, tiled=True),
    )
    product = jnp.einsum(
        "cik,cjk->cij", got_left[0], got_right[0], preferred_element_type=jnp.float32
    )
    returned = lax.all_to_all(
        product.astype(jnp.bfloat16)[None], "row", split_axis=2, concat_axis=0, tiled=True
    )
    tri_sum = jnp.transpose(returned.reshape(width, local_rows, tokens), (1, 2, 0))

    def finish_row(inputs):
        pair_row, summed, gate_row = inputs
        tri_norm = layer_norm(summed.astype(jnp.float32)).astype(jnp.bfloat16)
        update = jnp.dot(tri_norm, tri_out, preferred_element_type=jnp.float32)
        mid_pair = (pair_row.astype(jnp.float32) + gate_row * update).astype(jnp.bfloat16)
        mid_norm = layer_norm(mid_pair.astype(jnp.float32)).astype(jnp.bfloat16)
        att_all = jnp.dot(mid_norm, att_proj, preferred_element_type=jnp.float32)
        query = (att_all[:, :width] * scale).astype(jnp.bfloat16)
        key = att_all[:, width : 2 * width].astype(jnp.bfloat16)
        value = att_all[:, 2 * width : 3 * width].astype(jnp.bfloat16)
        att_gate = jax.nn.sigmoid(att_all[:, 3 * width :])
        pair_bias = jnp.dot(mid_norm, att_bias, preferred_element_type=jnp.float32).astype(
            jnp.bfloat16
        )
        return (mid_pair, query, key, value, att_gate, pair_bias)

    mid_pair, query, key, value, att_gate, pair_bias = lax.map(
        finish_row, (pair, tri_sum, out_gate)
    )
    bias_lay = jnp.transpose(pair_bias, (2, 0, 1))
    full_bias = lax.all_gather(bias_lay, "row", axis=1, tiled=True)
    logit_bias = chain_logits(full_bias, same_chain, chain, chain, mask_float)
    gated = attend(query, att_gate, key, value, logit_bias, head_count, head_size)
    projected_out = jnp.dot(gated.reshape(-1, width), att_out, preferred_element_type=jnp.float32)
    return (mid_pair.astype(jnp.float32) + projected_out.reshape(local_rows, tokens, width)).astype(
        jnp.bfloat16
    )


ROWS, TOKENS, WIDTH, PARTS, HEADS = 10, 160, 128, 16, 4
NEAR = PARTS // 2
SHARE = WIDTH // NEAR
TILES = 13
EARLY = 5
TAIL = TOKENS - 128


def dot(left, right, dims):
    return lax.dot_general(left, right, dims, preferred_element_type=F32)


def norm(values, axis):
    centred = values - jnp.mean(values, axis=axis, keepdims=True)
    spread = jnp.mean(centred * centred, axis=axis, keepdims=True)
    return (centred * lax.rsqrt(spread + 1e-05)).astype(BF16)


def pad_lanes(values):
    return jnp.concatenate(
        [values, jnp.zeros((values.shape[0], 128 - values.shape[1]), values.dtype)], axis=1
    )


def fused_kernel(
    *refs,
):
    outside, (out, *inside, loads) = refs[:10], refs[10:]
    held, scratch = inside[:10], inside[10:]
    fetches = [
        pltpu.make_async_copy(source, target, loads.at[k])
        for k, (source, target) in enumerate(zip(outside, held))
    ]
    for fetch in fetches:
        fetch.start()
    fused_body(fetches, out, *held, *scratch)


def fused_body(
    fetches,
    out,
    pair,
    tri_proj,
    mask_v,
    tri_gate,
    tri_out,
    bias_v,
    att_proj,
    chain_v,
    same_v,
    att_out,
    proj_t,
    normed,
    tails,
    send_l,
    recv_l,
    send_r,
    recv_r,
    left_m,
    left_t,
    right_m,
    right_t,
    sum_m,
    sum_t,
    send2,
    recv2,
    summed,
    gate,
    mid,
    mid_norm,
    bias_rows,
    send3,
    recv3,
    bias_m,
    bias_tl,
    logit,
    query,
    key,
    value,
    att_gate,
    sends,
    recvs,
    stores,
):
    me = lax.axis_index("row")

    place = lax.rem(me, NEAR)
    first = me - place

    def other(step):
        return lax.rem(me + step, PARTS)

    def near(step):
        return lax.rem(place + step, NEAR)

    barrier = pltpu.get_barrier_semaphore()

    @pl.loop(1, PARTS)
    def _(step):
        pl.semaphore_signal(
            barrier, inc=1, device_id={"row": other(step)}, device_id_type=pl.DeviceIdType.MESH
        )

    def copy_to(sent, phase, source, landing, slot, part):
        return pltpu.make_async_remote_copy(
            src_ref=source,
            dst_ref=landing.at[slot],
            send_sem=sends.at[sent, part],
            recv_sem=recvs.at[phase, slot],
            device_id={"row": part},
            device_id_type=pl.DeviceIdType.MESH,
        )

    def arrived(phase, landing, slot):
        return pltpu.make_async_remote_copy(
            src_ref=landing.at[slot],
            dst_ref=landing.at[slot],
            send_sem=sends.at[phase, slot],
            recv_sem=recvs.at[phase, slot],
            device_id={"row": other(1)},
            device_id_type=pl.DeviceIdType.MESH,
        )

    def right_copy(part):
        return copy_to(0, 0, send_r.at[lax.rem(part, NEAR)], recv_r, me, part)

    def sum_copy(slot):
        return copy_to(1, 1, send2.at[slot], recv2, place, first + slot)

    def bias_copy(part):
        return copy_to(2, 2, send3, recv3, me, part)

    def left_copy(slot):
        return copy_to(3, 3, send_l.at[slot], recv_l, place, first + slot)

    def passed_copy(slot):
        return copy_to(4, 2, recv3.at[across], recv3, across, first + slot)

    across = lax.rem(me + NEAR, PARTS)

    for fetch in fetches[:3]:
        fetch.wait()

    turned = tri_proj[...].astype(F32).T
    order = [turned[WIDTH * at : WIDTH * at + WIDTH] for at in (1, 3, 0, 2)]
    proj_t[...] = jnp.concatenate(order, axis=0).astype(BF16)
    mask_row = mask_v[...].astype(F32)
    token = lax.broadcasted_iota(jnp.int32, (1, TOKENS), 1)

    def project(i, row, side, send):
        weights = proj_t[2 * WIDTH * side : 2 * WIDTH * side + 2 * WIDTH]
        projected = dot(weights, row, NT)
        mine = jnp.where(token == me * ROWS + i, mask_row, 0.0)
        weight = mask_row * jnp.sum(mine, axis=1, keepdims=True)
        one = weight * jax.nn.sigmoid(projected[WIDTH:]) * projected[:WIDTH]
        send[:, i] = one[:, :128].astype(BF16).reshape(NEAR, SHARE, 128)
        tails[i] = one[:, 128:]

    def pack_tails(send):
        for tile in range(3):
            parts = [tails[i] for i in range(4 * tile, min(4 * tile + 4, ROWS))]
            packed = jnp.concatenate(parts, axis=1)
            if len(parts) < 4:
                packed = pad_lanes(packed)
            send[:, ROWS + tile] = packed.astype(BF16).reshape(NEAR, SHARE, 128)

    @pl.loop(0, ROWS, unroll=2)
    def _(i):
        row = norm(pair[i].astype(F32), 1)
        normed[i] = row
        project(i, row, 0, send_r)

    pack_tails(send_r)
    pl.semaphore_wait(barrier, PARTS - 1)

    @pl.loop(0, NEAR)
    def _(step):
        right_copy(lax.rem(across - place + near(step), PARTS)).start()

    @pl.loop(1, NEAR)
    def _(step):
        right_copy(first + near(step)).start()

    @pl.loop(0, ROWS, unroll=2)
    def _(i):
        project(i, normed[i], 1, send_l)

    pack_tails(send_l)

    @pl.loop(1, NEAR)
    def _(step):
        left_copy(near(step)).start()

    recv_l[place] = send_l[place]
    recv_r[me] = send_r[place]
    for fetch in fetches[3:]:
        fetch.wait()

    @pl.loop(0, ROWS, unroll=5)
    def _(i):
        gate[i] = jax.nn.sigmoid(jnp.dot(normed[i], tri_gate[...], preferred_element_type=F32))

    def unpack(landing, slot, main_f, tail_f):
        for i in range(ROWS):
            at = pl.ds(pl.multiple_of((slot * ROWS + i) * SHARE, SHARE), SHARE)
            main_f[at, :] = landing[slot, i].astype(F32)
            lane = TAIL * (i % 4)
            tail = landing[slot, ROWS + i // 4].astype(F32)[:, lane : lane + TAIL]
            tail_f[at, 0:TAIL] = tail

    @pl.loop(0, NEAR)
    def _(step):
        slot = near(step)

        @pl.when(step > 0)
        def _():
            arrived(3, recv_l, slot).wait_recv()
            arrived(0, recv_r, first + slot).wait_recv()

        unpack(recv_l, slot, left_m, left_t)
        unpack(recv_r, first + slot, right_m, right_t)

    @pl.loop(0, NEAR)
    def _(step):
        source = across - place + near(step)
        arrived(0, recv_r, source).wait_recv()
        unpack(recv_r, source, right_m, right_t)

    for c in range(SHARE):
        at_l, at_r = pl.ds(c, TOKENS // 2, stride=SHARE), pl.ds(c, TOKENS, stride=SHARE)
        main = dot(left_m[at_l, :].astype(BF16), right_m[at_r, :].astype(BF16), NT)
        tail = dot(
            left_t[at_l, :][:, :TAIL].astype(BF16), right_t[at_r, :][:, :TAIL].astype(BF16), NT
        )
        total = main + tail
        sum_m[at_l, :] = total[:, :128]
        sum_t[at_l, :] = pad_lanes(total[:, 128:])

    @pl.loop(1, NEAR + 1)
    def _(step):
        slot = near(step)
        at = pl.ds(pl.multiple_of(slot * ROWS * SHARE, ROWS * SHARE), ROWS * SHARE)
        send2[slot, 0:ROWS] = sum_m[at, :].astype(BF16).reshape(ROWS, SHARE, 128)
        rest = sum_t[at, :][:, :TAIL]
        for tile in range(3):
            parts = [rest[SHARE * i : SHARE * i + SHARE] for i in range(4 * tile, min(4 * tile + 4, ROWS))]
            packed = jnp.concatenate(parts, axis=1)
            if len(parts) < 4:
                packed = pad_lanes(packed)
            send2[slot, ROWS + tile] = packed.astype(BF16)

        @pl.when(step < NEAR)
        def _():
            sum_copy(slot).start()

    recv2[place] = send2[place]

    @pl.loop(1, NEAR)
    def _(step):
        arrived(1, recv2, near(step)).wait_recv()

    for i in range(ROWS):
        summed[i, :, 0:128] = recv2[:, i].astype(F32).reshape(WIDTH, 128)
        lane = TAIL * (i % 4)
        rest = recv2[:, ROWS + i // 4].astype(F32).reshape(WIDTH, 128)
        summed[i, :, 128:TOKENS] = rest[:, lane : lane + TAIL]

    high = bias_v[...].astype(BF16).astype(F32)
    none = jnp.zeros((HEADS, WIDTH), F32)
    bias_t = jnp.concatenate([high, none, bias_v[...] - high, none], axis=0).astype(BF16)

    @pl.loop(0, ROWS // 2, unroll=5)
    def _(pair_at):
        biases = []
        for half in range(2):
            i = pair_at * 2 + half
            tri_norm = norm(summed[i], 0)
            update = dot(tri_norm, tri_out[...], TN)
            mid_row = (pair[i].astype(F32) + gate[i] * update).astype(BF16)
            mid[i] = mid_row
            mid_n = norm(mid_row.astype(F32), 1)
            mid_norm[i] = mid_n
            bias = dot(bias_t, mid_n, NT)
            biases.append(bias[0:8] + bias[8:16])
        joined = jnp.concatenate([biases[0][0:HEADS], biases[1][0:HEADS]], axis=0)
        bias_rows[pl.ds(pl.multiple_of(pair_at * 8, 8), 8), :] = joined

    send3[0:32] = bias_rows[0:32, 0:128].astype(BF16)
    send3[32:48] = jnp.concatenate(
        [bias_rows[32:40, 0:128], jnp.zeros((8, 128), F32)], axis=0
    ).astype(BF16)
    last = jnp.concatenate([bias_rows[32:40, 128:TOKENS], jnp.zeros((8, TAIL), F32)], axis=0)
    send3[48:64] = pad_lanes(
        jnp.concatenate(
            [bias_rows[0:16, 128:TOKENS], bias_rows[16:32, 128:TOKENS], last], axis=1
        )
    ).astype(BF16)

    bias_copy(across).start()

    @pl.loop(1, NEAR)
    def _(step):
        bias_copy(first + near(step)).start()

    recv3[me] = send3[...]

    query_t = att_proj[:, 0:WIDTH].astype(F32).T.astype(BF16)
    channel = lax.broadcasted_iota(jnp.int32, (WIDTH, HEADS * TOKENS), 0) // (WIDTH // HEADS)
    lane = lax.broadcasted_iota(jnp.int32, (WIDTH, HEADS * TOKENS), 1)
    block = (lane >= channel * TOKENS) & (lane < channel * TOKENS + TOKENS)
    scale = (WIDTH // HEADS) ** (-0.5)

    def attention_inputs(i):
        mid_n = mid_norm[i]
        rest = jnp.dot(mid_n, att_proj[:, WIDTH:], preferred_element_type=F32)
        key[i] = rest[:, 0:WIDTH].astype(BF16)
        value[i] = rest[:, WIDTH : 2 * WIDTH].astype(BF16)
        att_gate[i] = jax.nn.sigmoid(rest[:, 2 * WIDTH :])
        wide = dot(query_t, jnp.concatenate([mid_n] * HEADS, axis=0), NT)
        query[i] = jnp.where(block, wide * scale, 0.0).astype(BF16)

    pl.loop(0, EARLY, unroll=5)(attention_inputs)
    arrived(2, recv3, across).wait_recv()

    @pl.loop(1, NEAR)
    def _(step):
        passed_copy(near(step)).start()

    pl.loop(EARLY, ROWS, unroll=5)(attention_inputs)

    ids = lax.broadcasted_iota(jnp.int32, (16, TOKENS), 0)
    one_hot = jnp.where(ids == chain_v[...], 1.0, 0.0).astype(BF16)
    same = dot(one_hot, one_hot, TN)
    absent = 10000.0 * (mask_row - 1.0)

    @pl.loop(0, PARTS)
    def _(step):
        source = other(step)

        @pl.when((step > 0) & (step != NEAR))
        def _():
            arrived(2, recv3, source).wait_recv()

    for source in range(PARTS):
        at = source * ROWS * HEADS
        got = recv3[source].astype(F32)
        bias_m[at : at + 40, :] = got[0:40]
        for t in range(3):
            size = 16 if t < 2 else 8
            bias_tl[at + 16 * t : at + 16 * t + size, 0:TAIL] = got[
                48 : 48 + size, TAIL * t : TAIL * t + TAIL
            ]

    mains, rests = [], []
    for h in range(HEADS):
        extra = same_v[0:1, h : h + 1] * same
        every = pl.ds(h, TOKENS, stride=HEADS)
        mains.append(bias_m[every, :] + extra[:, 0:128] + absent[:, 0:128])
        rest = bias_tl[every, :][:, :TAIL] + extra[:, 128:] + absent[:, 128:]
        rests.append(pad_lanes(rest))
    logit[0:128, :] = jnp.concatenate(mains, axis=0).T
    logit[128:TOKENS, :] = jnp.concatenate(rests, axis=0).T[0:TAIL]

    def row_out(i):
        return pltpu.make_async_copy(mid.at[i], out.at[i], stores.at[i])

    head_of = lax.broadcasted_iota(jnp.int32, (TOKENS, WIDTH), 1) // (WIDTH // HEADS)

    @pl.loop(0, ROWS, unroll=5)
    def _(i):
        scores = jnp.dot(key[i], query[i], preferred_element_type=F32) + logit[...]
        top = jnp.max(scores, axis=0, keepdims=True)
        exps = jnp.exp(scores - top)
        weight = (exps * (1.0 / jnp.sum(exps, axis=0, keepdims=True))).astype(BF16)
        mixes = dot(weight, value[i], TN)
        mixed = mixes[0:TOKENS]
        for h in range(1, HEADS):
            mixed = jnp.where(head_of == h, mixes[h * TOKENS : (h + 1) * TOKENS], mixed)
        gated = (att_gate[i] * mixed).astype(BF16)
        added = jnp.dot(gated, att_out[...], preferred_element_type=F32)
        mid[i] = (mid[i].astype(F32) + added).astype(BF16)
        row_out(i).start()

    @pl.loop(1, PARTS)
    def _(step):
        right_copy(other(step)).wait_send()

    bias_copy(across).wait_send()

    @pl.loop(0, ROWS)
    def _(i):
        row_out(i).wait()

    @pl.loop(1, NEAR)
    def _(step):
        slot = near(step)
        left_copy(slot).wait_send()
        sum_copy(slot).wait_send()
        bias_copy(first + slot).wait_send()
        passed_copy(slot).wait_send()


def per_device_fused(
    pair, mask, chain, tri_proj, tri_gate, tri_out, att_proj, att_bias, same_chain, att_out
):
    hbm = pl.BlockSpec(memory_space=pltpu.HBM)
    all_rows = (ROWS, TOKENS, WIDTH)
    inputs = (
        pair,
        tri_proj,
        mask.reshape(1, TOKENS),
        tri_gate,
        tri_out,
        att_bias.T,
        att_proj,
        chain.reshape(1, TOKENS),
        same_chain.reshape(1, HEADS),
        att_out,
    )
    return pl.pallas_call(
        fused_kernel,
        out_shape=jax.ShapeDtypeStruct(all_rows, BF16),
        in_specs=[hbm] * 10,
        out_specs=hbm,
        scratch_shapes=[pltpu.VMEM(each.shape, each.dtype) for each in inputs]
        + [
            pltpu.VMEM((4 * WIDTH, WIDTH), BF16),
            pltpu.VMEM(all_rows, BF16),
            pltpu.VMEM((ROWS, WIDTH, TAIL), F32),
            pltpu.VMEM((NEAR, TILES, SHARE, 128), BF16),
            pltpu.VMEM((NEAR, TILES, SHARE, 128), BF16),
            pltpu.VMEM((NEAR, TILES, SHARE, 128), BF16),
            pltpu.VMEM((PARTS, TILES, SHARE, 128), BF16),
            pltpu.VMEM((TOKENS // 2 * SHARE, 128), F32),
            pltpu.VMEM((TOKENS // 2 * SHARE, 128), F32),
            pltpu.VMEM((TOKENS * SHARE, 128), F32),
            pltpu.VMEM((TOKENS * SHARE, 128), F32),
            pltpu.VMEM((TOKENS // 2 * SHARE, 128), F32),
            pltpu.VMEM((TOKENS // 2 * SHARE, 128), F32),
            pltpu.VMEM((NEAR, TILES, SHARE, 128), BF16),
            pltpu.VMEM((NEAR, TILES, SHARE, 128), BF16),
            pltpu.VMEM((ROWS, WIDTH, TOKENS), F32),
            pltpu.VMEM(all_rows, F32),
            pltpu.VMEM(all_rows, BF16),
            pltpu.VMEM(all_rows, BF16),
            pltpu.VMEM((40, TOKENS), F32),
            pltpu.VMEM((64, 128), BF16),
            pltpu.VMEM((PARTS, 64, 128), BF16),
            pltpu.VMEM((TOKENS * HEADS, 128), F32),
            pltpu.VMEM((TOKENS * HEADS, 128), F32),
            pltpu.VMEM((TOKENS, HEADS * TOKENS), F32),
            pltpu.VMEM((ROWS, WIDTH, HEADS * TOKENS), BF16),
            pltpu.VMEM(all_rows, BF16),
            pltpu.VMEM(all_rows, BF16),
            pltpu.VMEM(all_rows, F32),
            pltpu.SemaphoreType.DMA((5, PARTS)),
            pltpu.SemaphoreType.DMA((5, PARTS)),
            pltpu.SemaphoreType.DMA((ROWS,)),
            pltpu.SemaphoreType.DMA((10,)),
        ],
        compiler_params=pltpu.CompilerParams(
            collective_id=0, has_side_effects=True, vmem_limit_bytes=64 * 1024 * 1024
        ),
    )(*inputs)


def per_device(pair, *others):
    fits = pair.shape == (ROWS, TOKENS, WIDTH) and lax.axis_size("row") == PARTS
    return (per_device_fused if fits else per_device_general)(pair, *others)


def solution(mesh):
    return jax.shard_map(
        per_device,
        mesh=mesh,
        in_specs=(
            P(("groups", "row"), None, None),
            P("groups"),
            P("groups"),
            P(),
            P(),
            P(),
            P(),
            P(),
            P(),
            P(),
        ),
        out_specs=P(("groups", "row"), None, None),
        check_vma=False,
    )
```
